128 devices in a mesh: replica: 8 (over y_lo, z), fsdp: 16 (over x, y_hi, core).
Axes of the slice: x: 4, y: 4 (y_hi: 2, y_lo: 2; y = y_hi * 2 + y_lo), z: 4, core: 2. Of those that a mesh axis runs over, the one named last changes fastest.
Arguments:
- activations: bfloat16 [8, 16, 256, 2304], P('replica', 'fsdp'), may hold values from -180 to 180
- labels: int32 [8, 16, 256], P('replica', 'fsdp'), may hold values from 0 to 255
- own_q: bfloat16 [8, 2304, 1024], P('replica', 'fsdp'), may hold values from -1 to 1
- own_k: bfloat16 [8, 2304, 512], P('replica', 'fsdp'), may hold values from -0.375 to 0.375
- own_v: bfloat16 [8, 2304, 512], P('replica', 'fsdp'), may hold values from -0.125 to 0.125
- own_o: bfloat16 [8, 1024, 2304], P('replica', 'fsdp'), may hold values from -0.1875 to 0.1875
- peer_q: bfloat16 [8, 2304, 1024], P('replica', 'fsdp'), may hold values from -1 to 1
- peer_k: bfloat16 [8, 2304, 512], P('replica', 'fsdp'), may hold values from -0.375 to 0.375
- peer_v: bfloat16 [8, 2304, 512], P('replica', 'fsdp'), may hold values from -0.125 to 0.125
- peer_o: bfloat16 [8, 1024, 2304], P('replica', 'fsdp'), may hold values from -0.1875 to 0.1875
- norm_gains: float32 [2, 2304], replicated, may hold values from 0.1 to 1.9
- label_head: bfloat16 [2304, 256], replicated, may hold values from -1 to 1
Outputs:
- token_loss: float32 [8, 16, 256], P('replica', 'fsdp')
- grad_q: float32 [8, 2304, 1024], P('replica', 'fsdp')
- grad_k: float32 [8, 2304, 512], P('replica', 'fsdp')
- grad_v: float32 [8, 2304, 512], P('replica', 'fsdp')
- grad_o: float32 [8, 1024, 2304], P('replica', 'fsdp')
The draws below stay inside these ranges and needn't reach their ends.
All inputs are finite; a program needn't handle non-finite values.
Results may differ from the reference program's by a relative error of at most 0.03.
The reference program's roundings to bfloat16 on the way count: a program that leaves them out, or rounds other values in their place, can miss the bound.
Values may be sent and summed in bfloat16 or wider, within the bound.
No kernel may reach another device: no remote copies, remote signals or barrier semaphores. Data moves between devices by JAX's collectives and lax.ppermute only.
A program may use at most 128 MiB of HBM per device.

```python
import math
import jax
import jax.numpy as jnp
from jax import lax

D = 2304
HEAD = 256
HQ = 4
HK = 2
LABELS = 256
SEQ = 256
SEQS_DEV = 1
QW = 1024
KW = 512
SEQS = 16
N_REPLICA = 8
N_FSDP = 16


def draw_activations(key, part):
    key = jax.random.fold_in(key, 11)
    key_base, key_rows, key_cols = jax.random.split(key, 3)
    row_scale = jnp.exp(jax.random.uniform(key_rows, (N_REPLICA, SEQS, SEQ, 1), jnp.float32, 0.0, math.log(10.0)))
    col_scale = jnp.exp(jax.random.uniform(key_cols, (D,), jnp.float32, math.log(0.3), math.log(3.0)))
    base = jnp.clip(jax.random.normal(key_base, (N_REPLICA, SEQS, SEQ, D), jnp.float32), -6.0, 6.0)
    return (base * row_scale * col_scale).astype(jnp.bfloat16)


def head_columns(key_pick, sharp):
    group_size = HQ // HK
    chosen = jax.random.randint(key_pick, (N_REPLICA, HK, 1), 0, group_size)
    within = jnp.arange(group_size, dtype=jnp.int32)[None, None, :]
    scales = jnp.where(within == chosen, jnp.float32(sharp), jnp.float32(1.0))
    scales = scales.reshape(N_REPLICA, 1, HQ)
    return jnp.repeat(scales, HEAD, axis=2)


def scaled_queries(base, key_pick, sharp):
    columns = head_columns(key_pick, sharp)
    return jnp.clip(base * columns / math.sqrt(D), -1.0, 1.0)


def draw_own_q(key, part):
    key = jax.random.fold_in(key, 21)
    key_pick, key_values = jax.random.split(key)
    base = jnp.clip(jax.random.normal(key_values, (N_REPLICA, D, HQ * HEAD), jnp.float32), -6.0, 6.0)
    return scaled_queries(base, key_pick, 8.0).astype(jnp.bfloat16)


def draw_peer_q(key, part):
    key = jax.random.fold_in(key, 22)
    key_pick, key_values = jax.random.split(key)
    base = jnp.clip(jax.random.normal(key_values, (N_REPLICA, D, HQ * HEAD), jnp.float32), -6.0, 6.0)
    return scaled_queries(base, key_pick, 8.0).astype(jnp.bfloat16)


def with_ends(array, rng, least, high):
    dims = array.shape
    spot = [jax.random.randint(jax.random.fold_in(rng, axis), (), 0, dims[axis]) for axis in range(len(dims))]
    array = array.at[tuple(spot)].set(least)
    longest = dims.index(max(dims))
    spot[longest] = (spot[longest] + 1) % dims[longest]
    return array.at[tuple(spot)].set(high)


def block_scale(rng, dims, cuts, smallest, largest):
    loudness, own = 1.0, jax.random.fold_in(rng, 6)
    for position, shards_of in cuts:
        heights = jnp.exp(jax.random.uniform(jax.random.fold_in(own, position), (shards_of,), jnp.float32, smallest / len(cuts), largest / len(cuts)))
        loudness = loudness * jnp.repeat(heights, dims[position] // shards_of).reshape([-1 if axis == position else 1 for axis in range(len(dims))])
    return loudness


def centred(key, extent, spread, reach, shards=(), kind=jnp.bfloat16):
    array = spread * jax.random.normal(key, extent, jnp.float32)
    if shards:
        array = array * block_scale(key, extent, shards, -0.22, 0.18)
    return jnp.clip(array, -reach, reach).astype(kind)


def setup_inputs(seed: int = 0) -> dict:
    streams_of = jax.random.split(jax.random.key(seed), 13)
    activations = draw_activations(jax.random.fold_in(streams_of[12], 71), 0)
    labels = with_ends(jax.random.randint(streams_of[1], (N_REPLICA, SEQS, SEQ), 0, LABELS), jax.random.fold_in(streams_of[1], 1), 0, LABELS - 1).astype(jnp.int32)
    own_q = draw_own_q(jax.random.fold_in(streams_of[12], 71), 0)
    own_k = centred(streams_of[3], (N_REPLICA, D, KW), (D // 9) ** -0.5, 0.375, ((0, 8), (1, 16)))
    own_v = centred(streams_of[4], (N_REPLICA, D, KW), D ** -0.5, 0.125, ((0, 8), (1, 16)))
    own_o = centred(streams_of[5], (N_REPLICA, QW, D), QW ** -0.5, 0.1875, ((0, 8), (1, 16)))
    peer_q = draw_peer_q(jax.random.fold_in(streams_of[12], 71), 0)
    peer_k = centred(streams_of[7], (N_REPLICA, D, KW), (D // 9) ** -0.5, 0.375, ((0, 8), (1, 16)))
    peer_v = centred(streams_of[8], (N_REPLICA, D, KW), D ** -0.5, 0.125, ((0, 8), (1, 16)))
    peer_o = centred(streams_of[9], (N_REPLICA, QW, D), QW ** -0.5, 0.1875, ((0, 8), (1, 16)))
    norm_gains = jnp.clip(1.0 + 0.18 * jax.random.normal(streams_of[10], (2, D), jnp.float32), 0.1, 1.9)
    label_head = centred(streams_of[11], (D, LABELS), 0.0625, 1.0)
    return {"activations": activations, "labels": labels, "own_q": own_q, "own_k": own_k, "own_v": own_v, "own_o": own_o, "peer_q": peer_q, "peer_k": peer_k, "peer_v": peer_v, "peer_o": peer_o, "norm_gains": norm_gains, "label_head": label_head}


EPSILON = 1e-06
ATTN_CAP = 50.0
LABEL_CAP = 30.0
MASKED = -1e+30

def rms_scale(values, gain):
    return values * lax.rsqrt(lax.optimization_barrier(jnp.mean(values * values, -1, keepdims=True)) + EPSILON) * gain

def attend(normed, weight_q, weight_k, weight_v, weight_o):
    seq_count, seq_length, feature_dim = normed.shape
    flattened = normed.reshape(seq_count * seq_length, feature_dim)
    head_count = weight_q.shape[1] // HEAD
    groups = weight_k.shape[1] // HEAD
    group_size = head_count // groups
    queries = jnp.dot(flattened, weight_q, preferred_element_type=jnp.float32).astype(jnp.bfloat16)
    queries = queries.reshape(seq_count, seq_length, groups, group_size, HEAD)
    key_rows = jnp.dot(flattened, weight_k, preferred_element_type=jnp.float32).astype(jnp.bfloat16)
    key_rows = key_rows.reshape(seq_count, seq_length, groups, HEAD)
    values = jnp.dot(flattened, weight_v, preferred_element_type=jnp.float32).astype(jnp.bfloat16)
    values = values.reshape(seq_count, seq_length, groups, HEAD)
    scores = jnp.einsum('bqgsd,bkgd->bgsqk', queries.astype(jnp.float32), key_rows.astype(jnp.float32))
    scores = ATTN_CAP * jnp.tanh(scores / math.sqrt(HEAD) / ATTN_CAP)
    causal = jnp.arange(seq_length)[:, None] >= jnp.arange(seq_length)[None, :]
    masked = jnp.where(causal, scores, jnp.float32(MASKED))
    top = lax.stop_gradient(lax.optimization_barrier(jnp.max(masked, -1, keepdims=True)))
    expwts = jnp.where(causal, jnp.exp(masked - top), jnp.float32(0.0))
    probabilities = (expwts / lax.optimization_barrier(jnp.sum(expwts, -1, keepdims=True))).astype(jnp.bfloat16)
    context = jnp.einsum('bgsqk,bkgd->bqgsd', probabilities.astype(jnp.float32), values.astype(jnp.float32))
    context = context.astype(jnp.bfloat16).reshape(seq_count * seq_length, head_count * HEAD)
    return jnp.dot(context, weight_o, preferred_element_type=jnp.float32).reshape(seq_count, seq_length, feature_dim)

def forward_logp(block_acts, weight_set, norm_gains, label_head):
    seq_count, seq_length, feature_dim = block_acts.shape
    widened = block_acts.astype(jnp.float32)
    normed = rms_scale(widened, norm_gains[0]).astype(jnp.bfloat16)
    hidden = widened + attend(normed, weight_set[0], weight_set[1], weight_set[2], weight_set[3])
    final_normed = rms_scale(hidden, norm_gains[1]).astype(jnp.bfloat16)
    logits = jnp.dot(final_normed.reshape(seq_count * seq_length, feature_dim), label_head, preferred_element_type=jnp.float32)
    logits = LABEL_CAP * jnp.tanh(logits / LABEL_CAP)
    log_probs = logits - jnp.log(lax.optimization_barrier(jnp.sum(jnp.exp(logits), -1, keepdims=True)))
    return log_probs.reshape(seq_count, seq_length, label_head.shape[1])

def token_losses(log_probs, peer_lp, block_labels):
    classes = jnp.arange(log_probs.shape[-1], dtype=jnp.int32)
    picked = lax.optimization_barrier(jnp.sum(jnp.where(block_labels[..., None] == classes, log_probs, jnp.float32(0.0)), -1))
    diverge = lax.optimization_barrier(jnp.sum(jnp.exp(peer_lp) * (peer_lp - log_probs), -1))
    return diverge - picked

def loss_parts(weight_set, block_acts, block_labels, peer_lp, norm_gains, label_head):
    log_probs = forward_logp(block_acts, weight_set, norm_gains, label_head)
    losses = token_losses(log_probs, peer_lp, block_labels)
    return (jnp.sum(losses) / losses.shape[1], losses)

def reference(activations, labels, own_q, own_k, own_v, own_o, peer_q, peer_k, peer_v, peer_o, norm_gains, label_head):
    all_losses, all_q, all_k, all_v, all_o = ([], [], [], [], [])
    for replica_idx in range(N_REPLICA):
        source = (replica_idx - 1) % N_REPLICA
        own_set = (own_q[replica_idx], own_k[replica_idx], own_v[replica_idx], own_o[replica_idx])
        peer_set = (peer_q[source], peer_k[source], peer_v[source], peer_o[source])
        grouped_acts = activations[replica_idx].reshape(N_FSDP, SEQS_DEV, SEQ, D)
        grouped_labels = labels[replica_idx].reshape(N_FSDP, SEQS_DEV, SEQ)

        def block_step(carry, scan_item, own_set=own_set, peer_set=peer_set):
            block_acts, block_labels = scan_item
            peer_lp = forward_logp(block_acts, peer_set, norm_gains, label_head)
            loss_sum, pullback, losses = jax.vjp(lambda weight_set: loss_parts(weight_set, block_acts, block_labels, peer_lp, norm_gains, label_head), own_set, has_aux=True)
            gradient, = pullback(jnp.ones_like(loss_sum))
            summed = tuple((acc + grad_part.astype(jnp.float32) for acc, grad_part in zip(carry, gradient)))
            return (summed, losses)
        start = tuple((jnp.zeros(weight.shape, jnp.float32) for weight in own_set))
        summed, losses = lax.scan(block_step, start, (grouped_acts, grouped_labels))
        all_losses.append(losses.reshape(SEQS, SEQ))
        all_q.append(summed[0])
        all_k.append(summed[1])
        all_v.append(summed[2])
        all_o.append(summed[3])
    return (jnp.stack(all_losses), jnp.stack(all_q), jnp.stack(all_k), jnp.stack(all_v), jnp.stack(all_o))
```

```python
import functools
import math

import jax
import jax.numpy as jnp
from jax import lax
from jax.experimental import pallas as pl
from jax.experimental.pallas import tpu as pltpu
from jax.sharding import PartitionSpec as P

SEQ, D, HEAD, HQ, HK, LABELS = 256, 2304, 256, 4, 2, 256
QKV_PANELS, O_PANELS = 8, 9
QKV_ROWS, O_ROWS = 144, 64
THIRD = 576
PACKED = 3 * THIRD
EPSILON = 1e-06
ATTN_CAP = 50.0
LABEL_CAP = 30.0
MASKED = -1e30
VMEM_LIMIT = 56 * 1024 * 1024
F32, BF16 = jnp.float32, jnp.bfloat16

N_FSDP = 16


def moved(value, target):
    return lax.ppermute(value, "fsdp", [(i, target(i)) for i in range(N_FSDP)])


def to_core(i):
    return i ^ 1


def to_y(i):
    return i ^ 2


def to_next_x(i):
    return (i + 4) % N_FSDP


def to_prev_x(i):
    return (i - 4) % N_FSDP


together = lax.optimization_barrier


def pack(w_q, w_k, w_v, w_o):
    panels = [w_q[:, HEAD * p : HEAD * (p + 1)] for p in range(4)]
    panels += [w_k[:, HEAD * p : HEAD * (p + 1)] for p in range(2)]
    panels += [w_v[:, HEAD * p : HEAD * (p + 1)] for p in range(2)]
    panels += [w_o[:, HEAD * p : HEAD * (p + 1)] for p in range(O_PANELS)]
    return jnp.concatenate(panels, 0)


def across_chips(shard):
    y0 = moved(shard, to_y)
    a1 = moved(shard, to_prev_x)
    a3 = moved(shard, to_next_x)
    return y0, a1, a3


def second_step(y0, a1, a3):
    return moved(a1, to_y), moved(y0, to_next_x), moved(a1, to_prev_x)


def third_step(o1, o3, a2):
    return (
        moved(a2[:THIRD], to_y),
        moved(o3[THIRD : 2 * THIRD], to_next_x),
        moved(o1[2 * THIRD :], to_prev_x),
    )


def whole(dx, dy):
    return (0, dx, dy, 0, 0, 3)


def swapped(arrays, metas):
    joined = jnp.concatenate(arrays, 0)
    met, row = [], 0
    for array, meta in zip(arrays, metas):
        for _, dx, dy, _, first, count in meta:
            met.append((row, dx, dy, 1, first, count))
        row += array.shape[0]
    return moved(joined, to_core), met


META = {
    "shard": [whole(0, 0)],
    "y0": [whole(0, 1)],
    "a1": [whole(1, 0)],
    "a3": [whole(3, 0)],
    "o1": [whole(1, 1)],
    "o3": [whole(3, 1)],
    "a2": [whole(2, 0)],
    "oA": [(0, 2, 1, 0, 0, 1)],
    "oB": [(0, 2, 1, 0, 1, 1)],
    "oC": [(0, 2, 1, 0, 2, 1)],
}


def rms(values, gain):
    mean = jnp.sum(values * values, -1, keepdims=True) * (1.0 / D)
    return values * lax.rsqrt(mean + EPSILON) * gain


def load_weights(position, metas, pieces, wqkv, wo, sems):
    x = position // 4
    y = (position // 2) % 2
    core = position % 2
    for ref, meta in zip(pieces, metas):
        for row, dx, dy, dc, first, count in meta:
            owner = ((x + dx) % 4) * 4
            owner = owner + (y if dy == 0 else 1 - y) * 2
            owner = owner + (core if dc == 0 else 1 - core)
            for third in range(first, first + count):
                at = row + THIRD * (third - first)
                if third < 2:
                    rows = pl.ds(pl.multiple_of(owner * QKV_ROWS, 16), QKV_ROWS)
                    for p in range(4):
                        pltpu.make_async_copy(
                            ref.at[pl.ds(at + QKV_ROWS * p, QKV_ROWS)],
                            wqkv.at[4 * third + p, rows],
                            sems.at[0],
                        ).start()
                else:
                    rows = pl.ds(pl.multiple_of(owner * O_ROWS, 16), O_ROWS)
                    for p in range(O_PANELS):
                        pltpu.make_async_copy(
                            ref.at[pl.ds(at + O_ROWS * p, O_ROWS)],
                            wo.at[p, rows],
                            sems.at[1],
                        ).start()


def wait_for(ref, sem):
    pltpu.make_async_copy(ref, ref, sem).wait()


def causal_mask():
    row = lax.broadcasted_iota(jnp.int32, (SEQ, SEQ), 0)
    col = lax.broadcasted_iota(jnp.int32, (SEQ, SEQ), 1)
    return row >= col


def nt(a, b):
    return lax.dot_general(a, b, (((1,), (1,)), ((), ())), preferred_element_type=F32)


def tn(a, b):
    return lax.dot_general(a, b, (((0,), (0,)), ((), ())), preferred_element_type=F32)


def nn(a, b):
    return jnp.dot(a, b, preferred_element_type=F32)


def probabilities(query, key, causal):
    capped = jnp.tanh(nt(query, key) * (1.0 / (math.sqrt(HEAD) * ATTN_CAP)))
    scores = jnp.where(causal, ATTN_CAP * capped, MASKED)
    top = jnp.max(scores, -1, keepdims=True)
    weights = jnp.where(causal, jnp.exp(scores - top), 0.0)
    return weights / jnp.sum(weights, -1, keepdims=True), capped


def layer(x_ref, gains_ref, head_ref, normed, qkv, context, hidden, wqkv, wo, sems):
    normed[...] = rms(x_ref[...].astype(F32), gains_ref[0:1, :]).astype(BF16)
    wait_for(wqkv, sems.at[0])

    def one_panel(p, carry):
        qkv[p] = nn(normed[...], wqkv[p]).astype(BF16)
        return carry

    lax.fori_loop(0, QKV_PANELS, one_panel, 0)
    causal = causal_mask()
    for h in range(HQ):
        group = h // (HQ // HK)
        probs, _ = probabilities(qkv[h], qkv[HQ + group], causal)
        context[:, HEAD * h : HEAD * (h + 1)] = nn(
            probs.astype(BF16), qkv[HQ + HK + group]
        ).astype(BF16)
    wait_for(wo, sems.at[1])

    def one_out(p, carry):
        cols = pl.ds(pl.multiple_of(p * HEAD, HEAD), HEAD)
        hidden[:, cols] = x_ref[:, cols].astype(F32) + nn(context[...], wo[p])
        return carry

    lax.fori_loop(0, O_PANELS, one_out, 0)
    final = rms(hidden[...], gains_ref[1:2, :]).astype(BF16)
    logits = LABEL_CAP * jnp.tanh(nn(final, head_ref[...]) * (1.0 / LABEL_CAP))
    return logits, logits - jnp.log(jnp.sum(jnp.exp(logits), -1, keepdims=True))


def own_kernel(metas, pos_ref, x_ref, gains_ref, head_ref, *refs):
    pieces, refs = refs[: len(metas)], refs[len(metas) :]
    nsel, csel, qkv, hidden, logits, wo, normed, context, wqkv, sems = refs
    load_weights(pos_ref[0], metas, pieces, wqkv, wo, sems)
    out, _ = layer(x_ref, gains_ref, head_ref, normed, qkv, context, hidden, wqkv, wo, sems)
    logits[...] = out
    for core in range(2):
        for chip in range(8):
            at = QKV_ROWS * (2 * chip + core)
            nsel[core, :, QKV_ROWS * chip : QKV_ROWS * (chip + 1)] = normed[:, at : at + QKV_ROWS]
            at = O_ROWS * (2 * chip + core)
            csel[core, :, O_ROWS * chip : O_ROWS * (chip + 1)] = context[:, at : at + O_ROWS]


def peer_kernel(metas, pos_ref, x_ref, gains_ref, head_ref, labels_ref, own_logits, own_hidden, *refs):
    pieces, refs = refs[: len(metas)], refs[len(metas) :]
    loss, dhidden, normed, qkv, context, hidden, wqkv, wo, sems = refs
    load_weights(pos_ref[0], metas, pieces, wqkv, wo, sems)
    _, peer_lp = layer(x_ref, gains_ref, head_ref, normed, qkv, context, hidden, wqkv, wo, sems)
    logits = own_logits[...]
    own_lp = logits - jnp.log(jnp.sum(jnp.exp(logits), -1, keepdims=True))
    peer = jnp.exp(peer_lp)
    hot = labels_ref[...] == lax.broadcasted_iota(jnp.int32, (SEQ, LABELS), 1)
    picked = jnp.sum(jnp.where(hot, own_lp, 0.0), -1, keepdims=True)
    loss[...] = jnp.sum(peer * (peer_lp - own_lp), -1, keepdims=True) - picked
    d_lp = (jnp.where(hot, 1.0, 0.0) + peer) * (-1.0 / SEQ)
    d_logits = d_lp - jnp.exp(own_lp) * jnp.sum(d_lp, -1, keepdims=True)
    capped = logits * (1.0 / LABEL_CAP)
    d_raw = (d_logits * (1.0 - capped * capped)).astype(BF16)
    d_final = nt(d_raw, head_ref[...]).astype(BF16).astype(F32) * gains_ref[1:2, :]
    own = own_hidden[...]
    scale = lax.rsqrt(jnp.sum(own * own, -1, keepdims=True) * (1.0 / D) + EPSILON)
    along = jnp.sum(d_final * own, -1, keepdims=True) * (1.0 / D)
    dhidden[...] = (d_final * scale - own * (scale * scale * scale * along)).astype(BF16)


def attention_back_kernel(dhidden, wo, qkv, dqkv, dcontext):
    dcontext[...] = jnp.zeros_like(dcontext)

    def one_panel(p, carry):
        cols = pl.ds(pl.multiple_of(p * HEAD, HEAD), HEAD)
        dcontext[...] += nt(dhidden[:, cols], wo[p])
        return carry

    lax.fori_loop(0, O_PANELS, one_panel, 0)
    causal = causal_mask()
    for group in range(HK):
        key, value = qkv[HQ + group], qkv[HQ + HK + group]
        d_key = jnp.zeros((SEQ, HEAD), F32)
        d_value = jnp.zeros((SEQ, HEAD), F32)
        for h in range(group * (HQ // HK), (group + 1) * (HQ // HK)):
            query = qkv[h]
            probs, capped = probabilities(query, key, causal)
            d_out = dcontext[:, HEAD * h : HEAD * (h + 1)].astype(BF16)
            d_value += tn(probs.astype(BF16), d_out)
            d_probs = nt(d_out, value).astype(BF16).astype(F32)
            d_scores = probs * (d_probs - jnp.sum(d_probs * probs, -1, keepdims=True))
            d_raw = (d_scores * (1.0 - capped * capped) * (1.0 / math.sqrt(HEAD))).astype(BF16)
            dqkv[h] = nn(d_raw, key).astype(BF16)
            d_key += tn(d_raw, query)
        dqkv[HQ + group] = d_key.astype(BF16)
        dqkv[HQ + HK + group] = d_value.astype(BF16)


CHIPS = [(0, 0), (1, 0), (2, 0), (3, 0), (0, 1), (1, 1), (2, 1), (3, 1)]


def chip_index(position, dx, dy):
    x = position // 4
    y = (position // 2) % 2
    return ((x + dx) % 4) * 2 + (y if dy == 0 else 1 - y)


def out_grad_kernel(pos_ref, mine, other, d_mine, d_other, *refs):
    outs, lhs = refs[:8], refs[8]
    lhs[:, 0:SEQ] = mine[...].T
    lhs[:, SEQ : 2 * SEQ] = other[...].T
    for out, (dx, dy) in zip(outs, CHIPS):
        rows = pl.ds(pl.multiple_of(chip_index(pos_ref[0], dx, dy) * O_ROWS, 16), O_ROWS)

        def one_panel(p, carry, out=out, rows=rows):
            cols = pl.ds(pl.multiple_of(p * HEAD, HEAD), HEAD)
            total = nn(lhs[rows, 0:SEQ], d_mine[:, cols])
            total += nn(lhs[rows, SEQ : 2 * SEQ], d_other[:, cols])
            out[pl.ds(pl.multiple_of(p * O_ROWS, 16), O_ROWS)] = total.astype(BF16)
            return carry

        lax.fori_loop(0, O_PANELS, one_panel, 0)


def qkv_grad_kernel(pos_ref, mine, other, d_mine, d_other, *refs):
    outs, lhs = refs[:8], refs[8]
    lhs[:, 0:SEQ] = mine[...].T
    lhs[:, SEQ : 2 * SEQ] = other[...].T
    for out, (dx, dy) in zip(outs, CHIPS):
        rows = pl.ds(pl.multiple_of(chip_index(pos_ref[0], dx, dy) * QKV_ROWS, 16), QKV_ROWS)

        def one_panel(p, carry, out=out, rows=rows):
            total = nn(lhs[rows, 0:SEQ], d_mine[p])
            total += nn(lhs[rows, SEQ : 2 * SEQ], d_other[p])
            out[pl.ds(pl.multiple_of(p * QKV_ROWS, 16), QKV_ROWS)] = total.astype(BF16)
            return carry

        lax.fori_loop(0, QKV_PANELS, one_panel, 0)


SMEM = pl.BlockSpec(memory_space=pltpu.SMEM)
VMEM = pl.BlockSpec(memory_space=pltpu.VMEM)
ANY = pl.BlockSpec(memory_space=pl.ANY)


def cost(flops, moved_bytes):
    return pl.CostEstimate(flops=flops, bytes_accessed=moved_bytes, transcendentals=0)


def shape(dims, kind=BF16):
    return jax.ShapeDtypeStruct(dims, kind)


def weight_scratch():
    return [
        pltpu.VMEM((QKV_PANELS, D, HEAD), BF16),
    ]


PARAMS = pltpu.CompilerParams(vmem_limit_bytes=VMEM_LIMIT)


def own_pass(position, x, gains, head, arrays, metas):
    return pl.pallas_call(
        functools.partial(own_kernel, metas),
        out_shape=[
            shape((2, SEQ, D // 2)),
            shape((2, SEQ, HQ * HEAD // 2)),
            shape((QKV_PANELS, SEQ, HEAD)),
            shape((SEQ, D), F32),
            shape((SEQ, LABELS), F32),
            shape((O_PANELS, HQ * HEAD, HEAD)),
        ],
        in_specs=[SMEM, VMEM, VMEM, VMEM] + [ANY] * len(arrays),
        out_specs=[VMEM] * 6,
        scratch_shapes=[
            pltpu.VMEM((SEQ, D), BF16),
            pltpu.VMEM((SEQ, HQ * HEAD), BF16),
            pltpu.VMEM((QKV_PANELS, D, HEAD), BF16),
            pltpu.SemaphoreType.DMA((2,)),
        ],
        compiler_params=PARAMS,
        cost_estimate=cost(4_000_000_000, 40_000_000),
        name="own_pass",
    )(position, x, gains, head, *arrays)


def peer_pass(position, x, gains, head, labels, own_logits, own_hidden, arrays, metas):
    return pl.pallas_call(
        functools.partial(peer_kernel, metas),
        out_shape=[shape((SEQ, 1), F32), shape((SEQ, D))],
        in_specs=[SMEM] + [VMEM] * 6 + [ANY] * len(arrays),
        out_specs=[VMEM] * 2,
        scratch_shapes=[
            pltpu.VMEM((SEQ, D), BF16),
            pltpu.VMEM((QKV_PANELS, SEQ, HEAD), BF16),
            pltpu.VMEM((SEQ, HQ * HEAD), BF16),
            pltpu.VMEM((SEQ, D), F32),
            pltpu.VMEM((QKV_PANELS, D, HEAD), BF16),
            pltpu.VMEM((O_PANELS, HQ * HEAD, HEAD), BF16),
            pltpu.SemaphoreType.DMA((2,)),
        ],
        compiler_params=PARAMS,
        cost_estimate=cost(4_000_000_000, 40_000_000),
        name="peer_pass",
    )(position, x, gains, head, labels, own_logits, own_hidden, *arrays)


def attention_back(dhidden, wo, qkv):
    return pl.pallas_call(
        attention_back_kernel,
        out_shape=shape((QKV_PANELS, SEQ, HEAD)),
        in_specs=[VMEM] * 3,
        out_specs=VMEM,
        scratch_shapes=[pltpu.VMEM((SEQ, HQ * HEAD), F32)],
        compiler_params=PARAMS,
        cost_estimate=cost(2_000_000_000, 16_000_000),
        name="attention_back",
    )(dhidden, wo, qkv)


def weight_grads(kernel, rows, panels, position, mine, other, d_mine, d_other, name):
    return pl.pallas_call(
        kernel,
        out_shape=[shape((rows * panels, HEAD))] * 8,
        in_specs=[SMEM] + [VMEM] * 4,
        out_specs=[VMEM] * 8,
        scratch_shapes=[pltpu.VMEM((8 * rows, 2 * SEQ), BF16)],
        compiler_params=PARAMS,
        cost_estimate=cost(2 * 8 * rows * 2 * SEQ * panels * HEAD, 10_000_000),
        name=name,
    )(position, mine, other, d_mine, d_other)


def added(first, *others):
    total = first.astype(F32)
    for value in others:
        total = total + value.astype(F32)
    return total


def reduce_scattered(blocks):
    s0, a1, a2, a3, o0, o1, o2, o3 = blocks
    t = o2.shape[0] // 3
    in_a, in_b, in_c = together(
        (
            moved(o2[:t], to_y),
            moved(o2[t : 2 * t], to_prev_x),
            moved(o2[2 * t :], to_next_x),
        )
    )
    a2 = jnp.concatenate([added(a2[:t], in_a).astype(BF16), a2[t:]], 0)
    o3 = jnp.concatenate([o3[:t], added(o3[t : 2 * t], in_b).astype(BF16), o3[2 * t :]], 0)
    o1 = jnp.concatenate([o1[: 2 * t], added(o1[2 * t :], in_c).astype(BF16)], 0)
    in_a1, in_o0, in_a1y = together(
        (moved(a2, to_next_x), moved(o3, to_prev_x), moved(o1, to_y))
    )
    a1 = added(a1, in_a1, in_a1y).astype(BF16)
    o0 = added(o0, in_o0).astype(BF16)
    last = together((moved(a1, to_next_x), moved(a3, to_prev_x), moved(o0, to_y)))
    return added(s0, *last)


def body(
    activations,
    labels,
    own_q,
    own_k,
    own_v,
    own_o,
    peer_q,
    peer_k,
    peer_v,
    peer_o,
    norm_gains,
    label_head,
):
    me = lax.axis_index("fsdp")
    core = me % 2
    position = me.astype(jnp.int32).reshape(1)
    x = activations[0, 0]

    own = pack(own_q[0], own_k[0], own_v[0], own_o[0])
    peer = pack(peer_q[0], peer_k[0], peer_v[0], peer_o[0])
    replicas = lax.axis_size("replica")
    peer = lax.ppermute(peer, "replica", [(i, (i + 1) % replicas) for i in range(replicas)])

    y0, a1, a3, own = together((*across_chips(own), own))
    o1, o3, a2 = together(second_step(y0, a1, a3))
    oA, oB, oC, peer = together((*third_step(o1, o3, a2), peer))
    names = ["shard", "y0", "a1", "a3", "o1", "o3", "a2", "oA", "oB", "oC"]
    arrays = [own, y0, a1, a3, o1, o3, a2, oA, oB, oC]
    metas = [META[n] for n in names]
    swap, met = swapped(arrays, metas)

    y0, a1, a3, peer, swap = together((*across_chips(peer), peer, swap))
    nsel, csel, qkv, hidden, logits, wo = own_pass(
        position, x, norm_gains, label_head, arrays + [swap], metas + [met]
    )
    n_mine = lax.dynamic_index_in_dim(nsel, core, 0, keepdims=False)
    n_other = moved(lax.dynamic_index_in_dim(nsel, 1 - core, 0, keepdims=False), to_core)
    c_mine = lax.dynamic_index_in_dim(csel, core, 0, keepdims=False)
    c_other = moved(lax.dynamic_index_in_dim(csel, 1 - core, 0, keepdims=False), to_core)

    swap1, met1 = swapped([peer, y0, a1, a3], [META[n] for n in names[:4]])
    o1, o3, a2, swap1 = together((*second_step(y0, a1, a3), swap1))
    swap2, met2 = swapped([o1, o3, a2], [META[n] for n in names[4:7]])
    oA, oB, oC, swap2 = together((*third_step(o1, o3, a2), swap2))
    swap3, met3 = swapped([oA, oB, oC], [META[n] for n in names[7:]])
    n_other, c_other, swap3 = together((n_other, c_other, swap3))

    loss, dhidden = peer_pass(
        position,
        x,
        norm_gains,
        label_head,
        labels[0, 0].reshape(SEQ, 1),
        logits,
        hidden,
        [peer, y0, a1, a3, o1, o3, a2, oA, oB, oC, swap1, swap2, swap3],
        metas + [met1, met2, met3],
    )
    d_other = moved(dhidden, to_core)
    dqkv = attention_back(dhidden, wo, qkv)
    out_blocks = weight_grads(
        out_grad_kernel, O_ROWS, O_PANELS, position, c_mine, c_other, dhidden, d_other, "out_grads"
    )
    dqkv_other = moved(dqkv, to_core)
    qkv_blocks = weight_grads(
        qkv_grad_kernel, QKV_ROWS, QKV_PANELS, position, n_mine, n_other, dqkv, dqkv_other, "qkv_grads"
    )
    grad_out = reduce_scattered(out_blocks).reshape(O_PANELS, O_ROWS, HEAD)
    grad_qkv = reduce_scattered(qkv_blocks).reshape(QKV_PANELS, QKV_ROWS, HEAD)

    def side_by_side(panels):
        return jnp.concatenate([panels[p] for p in range(panels.shape[0])], -1)[None]

    return (
        loss.reshape(1, 1, SEQ),
        side_by_side(grad_qkv[0:4]),
        side_by_side(grad_qkv[4:6]),
        side_by_side(grad_qkv[6:8]),
        side_by_side(grad_out),
    )


def solution(mesh):
    weights = P("replica", "fsdp", None)
    return jax.shard_map(
        body,
        mesh=mesh,
        in_specs=(P("replica", "fsdp", None, None), weights, *([weights] * 8), P(), P()),
        out_specs=(weights,) * 5,
        check_vma=False,
    )
```

```python
import functools
import math

import jax
import jax.numpy as jnp
from jax import lax
from jax.experimental import pallas as pl
from jax.experimental.pallas import tpu as pltpu
from jax.sharding import PartitionSpec as P

SEQ, D, HEAD, HQ, HK, LABELS = 256, 2304, 256, 4, 2, 256
QKV_PANELS, O_PANELS = 8, 9
QKV_ROWS, O_ROWS = 144, 64
THIRD = 576
PACKED = 3 * THIRD
EPSILON = 1e-06
ATTN_CAP = 50.0
LABEL_CAP = 30.0
MASKED = -1e30
F32, BF16 = jnp.float32, jnp.bfloat16

N_FSDP = 16


SMEM = pl.BlockSpec(memory_space=pltpu.SMEM)
VMEM = pl.BlockSpec(memory_space=pltpu.VMEM)
ANY = pl.BlockSpec(memory_space=pl.ANY)


def cost(flops, moved_bytes):
    return pl.CostEstimate(flops=flops, bytes_accessed=moved_bytes, transcendentals=0)


def shape(dims, kind=BF16):
    return jax.ShapeDtypeStruct(dims, kind)


def limit(mebibytes):
    return pltpu.CompilerParams(vmem_limit_bytes=mebibytes * 1024 * 1024)


def moved(value, target):
    return lax.ppermute(value, "fsdp", [(i, target(i)) for i in range(N_FSDP)])


def to_core(i):
    return i ^ 1


def to_y(i):
    return i ^ 2


def to_next_x(i):
    return (i + 4) % N_FSDP


def to_prev_x(i):
    return (i - 4) % N_FSDP


together = lax.optimization_barrier


def pack_kernel(w_q, w_k, w_v, w_o, out):
    row = 0
    for ref in (w_q, w_k, w_v, w_o):
        rows, cols = ref.shape
        for p in range(cols // HEAD):
            out[row : row + rows] = ref[:, HEAD * p : HEAD * (p + 1)]
            row += rows


def pack(w_q, w_k, w_v, w_o):
    return pl.pallas_call(
        pack_kernel,
        out_shape=shape((PACKED, HEAD)),
        in_specs=[VMEM] * 4,
        out_specs=VMEM,
        compiler_params=limit(8),
        cost_estimate=cost(0, 4_000_000),
        name="pack",
    )(w_q, w_k, w_v, w_o)


QKV_PART = QKV_PANELS * QKV_ROWS

SLOTS = [(0, 0), (3, 0), (0, 1), (1, 0), (2, 0), (3, 1), (1, 1), (2, 1)]
SLOT_ROWS = 2 * QKV_ROWS
OWN_EARLY, PEER_EARLY = 4, 3


def rms(values, gain):
    mean = jnp.sum(values * values, -1, keepdims=True) * (1.0 / D)
    return values * lax.rsqrt(mean + EPSILON) * gain


def chip_index(position, dx, dy):
    x = position // 4
    y = (position // 2) % 2
    return ((x + dx) % 4) * 2 + (y if dy == 0 else 1 - y)


def device_index(position, dx, dy, dc):
    core = position % 2
    return chip_index(position, dx, dy) * 2 + (core if dc == 0 else 1 - core)


def panel_copies(sources, refs, height, rows, target, sem):
    for panel, row in enumerate(rows):
        for piece, at, first, last in sources:
            if first <= row < last:
                pltpu.make_async_copy(
                    refs[piece].at[pl.ds(at + row - first, height)], target(panel), sem
                ).start()


def load_qkv(slots, refs, wqkv, sem):
    for slot, cores in enumerate(slots):
        for dc, sources in enumerate(cores):
            to = 2 * QKV_ROWS * slot + QKV_ROWS * dc
            panel_copies(
                sources,
                refs,
                QKV_ROWS,
                range(0, QKV_PART, QKV_ROWS),
                lambda p, to=to: wqkv.at[p, pl.ds(to, QKV_ROWS)],
                sem,
            )


def load_out(position, chips, slots, refs, wo, sem):
    for (dx, dy), cores in zip(chips, slots):
        for dc, sources in enumerate(cores):
            owner = device_index(position, dx, dy, dc)
            to = pl.ds(pl.multiple_of(owner * O_ROWS, 16), O_ROWS)
            panel_copies(
                sources,
                refs,
                O_ROWS,
                range(QKV_PART, PACKED, O_ROWS),
                lambda p, to=to: wo.at[to, pl.ds(HEAD * p, HEAD)],
                sem,
            )


def wait_for(ref, sem):
    pltpu.make_async_copy(ref, ref, sem).wait()


def causal_mask():
    row = lax.broadcasted_iota(jnp.int32, (SEQ, SEQ), 0)
    col = lax.broadcasted_iota(jnp.int32, (SEQ, SEQ), 1)
    return row >= col


def nt(a, b):
    return lax.dot_general(a, b, (((1,), (1,)), ((), ())), preferred_element_type=F32)


def tn(a, b):
    return lax.dot_general(a, b, (((0,), (0,)), ((), ())), preferred_element_type=F32)


def nn(a, b):
    return jnp.dot(a, b, preferred_element_type=F32)


def probabilities(query, key, causal):
    capped = jnp.tanh(nt(query, key) * (1.0 / (math.sqrt(HEAD) * ATTN_CAP)))
    scores = jnp.where(causal, ATTN_CAP * capped, MASKED)
    top = jnp.max(scores, -1, keepdims=True)
    weights = jnp.where(causal, jnp.exp(scores - top), 0.0)
    return weights / jnp.sum(weights, -1, keepdims=True), capped


def prepare_kernel(pos_ref, x_ref, gains_ref, *refs):
    parts, (n_mine, n_send, turned, ordered) = refs[:4], refs[4:]
    normed = rms(x_ref[...].astype(F32), gains_ref[0:1, :]).astype(BF16)
    turned[...] = normed.T

    def rows_of(device):
        return turned[pl.ds(pl.multiple_of(device * QKV_ROWS, 16), QKV_ROWS)]

    position = pos_ref[0]
    for slot, (dx, dy) in enumerate(SLOTS):
        for dc in range(2):
            to = SLOT_ROWS * slot + QKV_ROWS * dc
            ordered[to : to + QKV_ROWS] = rows_of(device_index(position, dx, dy, dc))
    for split, early, late in ((OWN_EARLY, *parts[:2]), (PEER_EARLY, *parts[2:])):
        early[...] = ordered[0 : SLOT_ROWS * split].T
        late[...] = ordered[SLOT_ROWS * split :].T
    core = position % 2
    for chip in range(8):
        to = slice(QKV_ROWS * chip, QKV_ROWS * (chip + 1))
        n_mine[to] = rows_of(2 * chip + core)
        n_send[to] = rows_of(2 * chip + 1 - core)


def early_kernel(slots, normed, *refs):
    pieces, (acc, wqkv, sem) = refs[:-3], refs[-3:]
    load_qkv(slots, pieces, wqkv, sem)
    wait_for(wqkv, sem)

    def one_panel(p, carry):
        acc[p] = nn(normed[...], wqkv[p])
        return carry

    lax.fori_loop(0, QKV_PANELS, one_panel, 0)


def layer(position, early, slots, x_ref, gains_ref, head_ref, normed, acc, pieces, qkv, context, hidden, wqkv, wo, sems):
    load_qkv(slots[early:], pieces, wqkv, sems.at[0])
    load_out(position, SLOTS, slots, pieces, wo, sems.at[1])
    wait_for(wqkv, sems.at[0])

    def one_panel(p, carry):
        qkv[p] = (acc[p] + nn(normed[...], wqkv[p])).astype(BF16)
        return carry

    lax.fori_loop(0, QKV_PANELS, one_panel, 0)
    causal = causal_mask()
    for h in range(HQ):
        group = h // (HQ // HK)
        probs, _ = probabilities(qkv[h], qkv[HQ + group], causal)
        context[:, HEAD * h : HEAD * (h + 1)] = nn(
            probs.astype(BF16), qkv[HQ + HK + group]
        ).astype(BF16)
    wait_for(wo, sems.at[1])

    def one_out(p, carry):
        cols = pl.ds(pl.multiple_of(p * HEAD, HEAD), HEAD)
        hidden[:, cols] = x_ref[:, cols].astype(F32) + nn(context[...], wo[:, cols])
        return carry

    lax.fori_loop(0, O_PANELS, one_out, 0)
    final = rms(hidden[...], gains_ref[1:2, :]).astype(BF16)
    logits = LABEL_CAP * jnp.tanh(nn(final, head_ref[...]) * (1.0 / LABEL_CAP))
    return logits, logits - jnp.log(jnp.sum(jnp.exp(logits), -1, keepdims=True))


def own_kernel(slots, pos_ref, x_ref, gains_ref, head_ref, normed, acc, *refs):
    pieces, refs = refs[:-10], refs[-10:]
    c_mine, c_send, qkv, hidden, logits, wo, context, turned, wqkv, sems = refs
    position = pos_ref[0]
    logits[...], _ = layer(
        position, OWN_EARLY, slots, x_ref, gains_ref, head_ref, normed, acc, pieces, qkv, context, hidden, wqkv, wo, sems
    )
    turned[...] = context[...].T
    core = position % 2
    for chip in range(8):
        to = slice(O_ROWS * chip, O_ROWS * (chip + 1))
        at = pl.multiple_of((2 * chip + core) * O_ROWS, 16)
        c_mine[to] = turned[pl.ds(at, O_ROWS)]
        at = pl.multiple_of((2 * chip + 1 - core) * O_ROWS, 16)
        c_send[to] = turned[pl.ds(at, O_ROWS)]


def peer_kernel(
    slots, pos_ref, x_ref, gains_ref, head_ref, normed, acc, labels_ref, own_logits, own_hidden, *refs
):
    pieces, refs = refs[:-8], refs[-8:]
    loss, dhidden, qkv, context, hidden, wqkv, wo, sems = refs
    _, peer_lp = layer(
        pos_ref[0], PEER_EARLY, slots, x_ref, gains_ref, head_ref, normed, acc, pieces, qkv, context, hidden, wqkv, wo, sems
    )
    logits = own_logits[...]
    own_lp = logits - jnp.log(jnp.sum(jnp.exp(logits), -1, keepdims=True))
    peer = jnp.exp(peer_lp)
    hot = labels_ref[...] == lax.broadcasted_iota(jnp.int32, (SEQ, LABELS), 1)
    picked = jnp.sum(jnp.where(hot, own_lp, 0.0), -1, keepdims=True)
    loss[...] = jnp.sum(peer * (peer_lp - own_lp), -1, keepdims=True) - picked
    d_lp = (jnp.where(hot, 1.0, 0.0) + peer) * (-1.0 / SEQ)
    d_logits = d_lp - jnp.exp(own_lp) * jnp.sum(d_lp, -1, keepdims=True)
    capped = logits * (1.0 / LABEL_CAP)
    d_raw = (d_logits * (1.0 - capped * capped)).astype(BF16)
    d_final = nt(d_raw, head_ref[...]).astype(BF16).astype(F32) * gains_ref[1:2, :]
    own = own_hidden[...]
    scale = lax.rsqrt(jnp.sum(own * own, -1, keepdims=True) * (1.0 / D) + EPSILON)
    along = jnp.sum(d_final * own, -1, keepdims=True) * (1.0 / D)
    dhidden[...] = (d_final * scale - own * (scale * scale * scale * along)).astype(BF16)


def attention_back_kernel(dhidden, wo, qkv, dqkv):
    causal = causal_mask()
    for group in range(HK):
        key, value = qkv[HQ + group], qkv[HQ + HK + group]
        d_key = jnp.zeros((SEQ, HEAD), F32)
        d_value = jnp.zeros((SEQ, HEAD), F32)
        for h in range(group * (HQ // HK), (group + 1) * (HQ // HK)):
            query = qkv[h]
            probs, capped = probabilities(query, key, causal)
            d_out = nt(dhidden[...], wo[HEAD * h : HEAD * (h + 1), :]).astype(BF16)
            d_value += tn(probs.astype(BF16), d_out)
            d_probs = nt(d_out, value).astype(BF16).astype(F32)
            d_scores = probs * (d_probs - jnp.sum(d_probs * probs, -1, keepdims=True))
            d_raw = (d_scores * (1.0 - capped * capped) * (1.0 / math.sqrt(HEAD))).astype(BF16)
            dqkv[h] = nn(d_raw, key).astype(BF16)
            d_key += tn(d_raw, query)
        dqkv[HQ + group] = d_key.astype(BF16)
        dqkv[HQ + HK + group] = d_value.astype(BF16)


CHIPS = [(0, 0), (1, 0), (2, 0), (3, 0), (0, 1), (1, 1), (2, 1), (3, 1)]


def block_outs(outs):
    return [[o] for o in outs[:6]] + [list(outs[6:9])] + [[outs[9]]]


def hand_out(position, outs, whole_blocks):
    for parts, (dx, dy) in zip(block_outs(outs), CHIPS):
        at = chip_index(position, dx, dy)
        row = 0
        for part in parts:
            part[...] = whole_blocks[at, row : row + part.shape[0]]
            row += part.shape[0]


def out_grad_kernel(pos_ref, mine, other, d_mine, d_other, *refs):
    outs, (lhs, rhs, blocks) = refs[:10], refs[10:]
    lhs[:, 0:SEQ], lhs[:, SEQ : 2 * SEQ] = mine[...], other[...]
    rhs[0:SEQ], rhs[SEQ : 2 * SEQ] = d_mine[...], d_other[...]

    def one_panel(p, carry):
        cols = pl.ds(pl.multiple_of(p * HEAD, HEAD), HEAD)
        rows = pl.ds(pl.multiple_of(p * O_ROWS, 16), O_ROWS)
        total = nn(lhs[...], rhs[:, cols]).astype(BF16)
        for chip in range(8):
            blocks[chip, rows] = total[O_ROWS * chip : O_ROWS * (chip + 1)]
        return carry

    lax.fori_loop(0, O_PANELS, one_panel, 0)
    hand_out(pos_ref[0], outs, blocks)


def qkv_grad_kernel(pos_ref, mine, other, d_mine, d_other, *refs):
    outs, (lhs, rhs, blocks) = refs[:10], refs[10:]
    lhs[:, 0:SEQ], lhs[:, SEQ : 2 * SEQ] = mine[...], other[...]
    rhs[:, 0:SEQ], rhs[:, SEQ : 2 * SEQ] = d_mine[...], d_other[...]

    def one_panel(p, carry):
        rows = pl.ds(pl.multiple_of(p * QKV_ROWS, 16), QKV_ROWS)
        total = nn(lhs[...], rhs[p]).astype(BF16)
        for chip in range(8):
            blocks[chip, rows] = total[QKV_ROWS * chip : QKV_ROWS * (chip + 1)]
        return carry

    lax.fori_loop(0, QKV_PANELS, one_panel, 0)
    hand_out(pos_ref[0], outs, blocks)


def prepare(position, x, gains):
    return pl.pallas_call(
        prepare_kernel,
        out_shape=[
            shape((SEQ, SLOT_ROWS * count))
            for count in (OWN_EARLY, 8 - OWN_EARLY, PEER_EARLY, 8 - PEER_EARLY)
        ]
        + [shape((D // 2, SEQ))] * 2,
        in_specs=[SMEM, VMEM, VMEM],
        out_specs=[VMEM] * 6,
        scratch_shapes=[pltpu.VMEM((D, SEQ), BF16)] * 2,
        compiler_params=limit(20),
        cost_estimate=cost(10_000_000, 10_000_000),
        name="prepare",
    )(position, x, gains)


def some_wqkv(count):
    return pltpu.VMEM((QKV_PANELS, SLOT_ROWS * count, HEAD), BF16)


def early_pass(normed, arrays, slots):
    return pl.pallas_call(
        functools.partial(early_kernel, slots),
        out_shape=shape((QKV_PANELS, SEQ, HEAD), F32),
        in_specs=[VMEM] + [ANY] * len(arrays),
        out_specs=VMEM,
        scratch_shapes=[some_wqkv(len(slots)), pltpu.SemaphoreType.DMA],
        compiler_params=limit(14),
        cost_estimate=cost(1_200_000_000, 20_000_000),
        name="early_pass",
    )(normed, *arrays)


def own_pass(position, x, gains, head, normed, acc, arrays, slots):
    return pl.pallas_call(
        functools.partial(own_kernel, slots),
        out_shape=[
            shape((HQ * HEAD // 2, SEQ)),
            shape((HQ * HEAD // 2, SEQ)),
            shape((QKV_PANELS, SEQ, HEAD)),
            shape((SEQ, D), F32),
            shape((SEQ, LABELS), F32),
            shape((HQ * HEAD, D)),
        ],
        in_specs=[SMEM] + [VMEM] * 5 + [ANY] * len(arrays),
        out_specs=[VMEM] * 6,
        scratch_shapes=[
            pltpu.VMEM((SEQ, HQ * HEAD), BF16),
            pltpu.VMEM((HQ * HEAD, SEQ), BF16),
            some_wqkv(8 - OWN_EARLY),
            pltpu.SemaphoreType.DMA((2,)),
        ],
        compiler_params=limit(32),
        cost_estimate=cost(3_000_000_000, 30_000_000),
        name="own_pass",
    )(position, x, gains, head, normed, acc, *arrays)


def peer_pass(position, x, gains, head, normed, acc, labels, own_logits, own_hidden, arrays, slots):
    return pl.pallas_call(
        functools.partial(peer_kernel, slots),
        out_shape=[shape((SEQ, 1), F32), shape((SEQ, D))],
        in_specs=[SMEM] + [VMEM] * 8 + [ANY] * len(arrays),
        out_specs=[VMEM] * 2,
        scratch_shapes=[
            pltpu.VMEM((QKV_PANELS, SEQ, HEAD), BF16),
            pltpu.VMEM((SEQ, HQ * HEAD), BF16),
            pltpu.VMEM((SEQ, D), F32),
            some_wqkv(8 - PEER_EARLY),
            pltpu.VMEM((HQ * HEAD, D), BF16),
            pltpu.SemaphoreType.DMA((2,)),
        ],
        compiler_params=limit(38),
        cost_estimate=cost(3_000_000_000, 30_000_000),
        name="peer_pass",
    )(position, x, gains, head, normed, acc, labels, own_logits, own_hidden, *arrays)


def attention_back(dhidden, wo, qkv):
    return pl.pallas_call(
        attention_back_kernel,
        out_shape=shape((QKV_PANELS, SEQ, HEAD)),
        in_specs=[VMEM] * 3,
        out_specs=VMEM,
        compiler_params=limit(20),
        cost_estimate=cost(2_000_000_000, 16_000_000),
        name="attention_back",
    )(dhidden, wo, qkv)


def weight_grads(kernel, rows, panels, rhs, position, mine, other, d_mine, d_other, name):
    block = rows * panels
    return pl.pallas_call(
        kernel,
        out_shape=[shape((block, HEAD))] * 6 + [shape((block // 3, HEAD))] * 3 + [shape((block, HEAD))],
        in_specs=[SMEM] + [VMEM] * 4,
        out_specs=[VMEM] * 10,
        scratch_shapes=[
            pltpu.VMEM((8 * rows, 2 * SEQ), BF16),
            pltpu.VMEM(rhs, BF16),
            pltpu.VMEM((8, block, HEAD), BF16),
        ],
        compiler_params=limit(28),
        cost_estimate=cost(2 * 8 * rows * 2 * SEQ * panels * HEAD, 10_000_000),
        name=name,
    )(position, mine, other, d_mine, d_other)


def third_added_kernel(a2, o3, o1, in_a, in_b, in_c, a2_out, o3_out, o1_out):
    t = in_a.shape[0]
    for third, (value, more, out) in enumerate(
        ((a2, in_a, a2_out), (o3, in_b, o3_out), (o1, in_c, o1_out))
    ):
        for part in range(3):
            rows = slice(t * part, t * (part + 1))
            if part == third:
                out[rows] = (value[rows].astype(F32) + more[...].astype(F32)).astype(BF16)
            else:
                out[rows] = value[rows]


def next_added_kernel(a1, o0, in_x, in_y, in_o0, a1_out, o0_out):
    total = a1[...].astype(F32) + in_x[...].astype(F32) + in_y[...].astype(F32)
    a1_out[...] = total.astype(BF16)
    o0_out[...] = (o0[...].astype(F32) + in_o0[...].astype(F32)).astype(BF16)


def summed_kernel(rows, *refs):
    parts, outs = refs[:4], refs[4:]
    row = 0
    for out in outs:
        for p in range(out.shape[1] // HEAD):
            at = slice(row, row + rows)
            total = parts[0][at].astype(F32)
            for part in parts[1:]:
                total += part[at].astype(F32)
            out[:, HEAD * p : HEAD * (p + 1)] = total
            row += rows


def elementwise(kernel, outs, name, *values):
    return pl.pallas_call(
        kernel,
        out_shape=outs,
        in_specs=[VMEM] * len(values),
        out_specs=[VMEM] * len(outs),
        compiler_params=limit(12),
        cost_estimate=cost(1_000_000, 4_000_000),
        name=name,
    )(*values)


def reduce_first(blocks):
    return moved(blocks[6], to_y), moved(blocks[7], to_prev_x), moved(blocks[8], to_next_x)


def add_thirds(blocks, incoming):
    a2, o3, o1 = blocks[2], blocks[9], blocks[5]
    outs = [shape(a2.shape)] * 3
    return elementwise(third_added_kernel, outs, "add_thirds", a2, o3, o1, *incoming)


def reduce_rest(blocks, added, rows, widths):
    s0, a1, _, a3, o0, *_ = blocks
    a2, o3, o1 = added
    one = shape(s0.shape)
    in_x, in_o0, in_y = together((moved(a2, to_next_x), moved(o3, to_prev_x), moved(o1, to_y)))
    a1, o0 = elementwise(next_added_kernel, [one] * 2, "add_next", a1, o0, in_x, in_y, in_o0)
    last = together((moved(a1, to_next_x), moved(a3, to_prev_x), moved(o0, to_y)))
    outs = [shape((rows, width), F32) for width in widths]
    return elementwise(functools.partial(summed_kernel, rows), outs, "add_last", s0, *last)


def body(
    activations,
    labels,
    own_q,
    own_k,
    own_v,
    own_o,
    peer_q,
    peer_k,
    peer_v,
    peer_o,
    norm_gains,
    label_head,
):
    me = lax.axis_index("fsdp")
    position = me.astype(jnp.int32).reshape(1)
    x = activations[0, 0]
    replicas = lax.axis_size("replica")

    own = pack(own_q[0], own_k[0], own_v[0], own_o[0])
    peer = pack(peer_q[0], peer_k[0], peer_v[0], peer_o[0])

    a1, a3 = moved(own, to_prev_x), moved(own, to_next_x)
    peer = lax.ppermute(peer, "replica", [(i, (i + 1) % replicas) for i in range(replicas)])
    prepared = prepare(position, x, norm_gains)
    a1, a3, peer, own, prepared = together((a1, a3, peer, own, prepared))
    n_early, n_late, n_peer_early, n_peer_late, n_mine, n_send = prepared

    y0, a2, p_a3 = moved(own, to_y), moved(a1, to_prev_x), moved(peer, to_next_x)
    n_other = moved(n_send, to_core)
    joined = jnp.concatenate([own, a3, a1], 0)
    y0, a2, p_a3, joined, n_other = together((y0, a2, p_a3, joined, n_other))

    p_y0, o3, o1 = moved(peer, to_y), moved(y0, to_next_x), moved(y0, to_prev_x)
    swap_first, swap_a2 = moved(joined, to_core), moved(a2, to_core)
    p_y0, o3, o1, swap_first, swap_a2 = together((p_y0, o3, o1, swap_first, swap_a2))

    o2, p_a1, p_o3 = moved(a2, to_y), moved(peer, to_prev_x), moved(p_y0, to_next_x)
    swap_y0, swap_o3 = moved(y0, to_core), moved(o3, to_core)

    def all_of(piece, at=0):
        return [(piece, at, 0, PACKED)]

    own_slots = [
        (all_of(0), all_of(4, 0)),
        (all_of(1), all_of(4, PACKED)),
        (all_of(2), all_of(5)),
        (all_of(3), all_of(4, 2 * PACKED)),
        (all_of(6), all_of(10)),
        (all_of(7), all_of(11)),
        (all_of(8), all_of(12)),
        (all_of(9), all_of(13)),
    ]
    acc = early_pass(n_early, [own, a3, y0, a1, swap_first, swap_y0], own_slots[:OWN_EARLY])
    joined = jnp.concatenate([peer, p_a3, p_y0], 0)
    o2, p_a1, p_o3, swap_o3, joined, acc = together((o2, p_a1, p_o3, swap_o3, joined, acc))

    p_o1, p_a2, p_o2 = moved(p_a1, to_y), moved(p_a1, to_prev_x), moved(p_o3, to_next_x)
    swap_o1, swap_o2 = moved(o1, to_core), moved(o2, to_core)
    p_swap_first = moved(joined, to_core)
    c_mine, c_send, qkv, hidden, logits, wo = own_pass(
        position,
        x,
        norm_gains,
        label_head,
        n_late,
        acc,
        [own, a3, y0, a1, swap_first, swap_y0, a2, o3, o1, o2, swap_a2, swap_o3, swap_o1, swap_o2],
        own_slots,
    )
    p_o1, p_a2, p_o2, p_swap_first, c_send, hidden = together(
        (p_o1, p_a2, p_o2, p_swap_first, c_send, hidden)
    )

    late = [p_a1, p_a2, p_o3, p_o1, p_o2]
    swap_late = [moved(piece, to_core) for piece in late]
    c_other = moved(c_send, to_core)
    peer_slots = [(all_of(i), all_of(3, PACKED * i)) for i in range(PEER_EARLY)]
    p_acc = early_pass(n_peer_early, [peer, p_a3, p_y0, p_swap_first], peer_slots)
    peer_slots = peer_slots + [(all_of(4 + i), all_of(9 + i)) for i in range(8 - PEER_EARLY)]
    loss, dhidden = peer_pass(
        position,
        x,
        norm_gains,
        label_head,
        n_peer_late,
        p_acc,
        labels[0, 0].reshape(SEQ, 1),
        logits,
        hidden,
        [peer, p_a3, p_y0, p_swap_first, *late, *swap_late],
        peer_slots,
    )
    d_other = moved(dhidden, to_core)
    dqkv = attention_back(dhidden, wo, qkv)
    dqkv_other = moved(dqkv, to_core)
    out_blocks = weight_grads(
        out_grad_kernel,
        *(O_ROWS, O_PANELS, (2 * SEQ, D)),
        *(position, c_mine, c_other, dhidden, d_other, "out_grads"),
    )
    dqkv, dqkv_other, *out_blocks = together((dqkv, dqkv_other, *out_blocks))
    qkv_blocks = weight_grads(
        qkv_grad_kernel,
        *(QKV_ROWS, QKV_PANELS, (QKV_PANELS, 2 * SEQ, HEAD)),
        *(position, n_mine, n_other, dqkv, dqkv_other, "qkv_grads"),
    )
    in_a, in_b, in_c, *qkv_blocks = together((*reduce_first(out_blocks), *qkv_blocks))
    added, qkv_blocks = together((add_thirds(out_blocks, (in_a, in_b, in_c)), qkv_blocks))
    (grad_out,) = reduce_rest(out_blocks, added, O_ROWS, [D])
    added = add_thirds(qkv_blocks, together(reduce_first(qkv_blocks)))
    grads = reduce_rest(qkv_blocks, added, QKV_ROWS, [HQ * HEAD, HK * HEAD, HK * HEAD])
    return (loss.reshape(1, 1, SEQ), *[grad[None] for grad in grads], grad_out[None])


def solution(mesh):
    weights = P("replica", "fsdp", None)
    return jax.shard_map(
        body,
        mesh=mesh,
        in_specs=(P("replica", "fsdp", None, None), weights, *([weights] * 8), P(), P()),
        out_specs=(weights,) * 5,
        check_vma=False,
    )
```

```python
import functools
import math

import jax
import jax.numpy as jnp
from jax import lax
from jax.experimental import pallas as pl
from jax.experimental.pallas import tpu as pltpu
from jax.sharding import PartitionSpec as P

SEQ, D, HEAD, HQ, HK, LABELS = 256, 2304, 256, 4, 2, 256
QKV_PANELS, O_PANELS = 8, 9
QKV_ROWS, O_ROWS = 144, 64
THIRD = 576
PACKED = 3 * THIRD
EPSILON = 1e-06
ATTN_CAP = 50.0
LABEL_CAP = 30.0
MASKED = -1e30
F32, BF16 = jnp.float32, jnp.bfloat16

N_FSDP = 16


SMEM = pl.BlockSpec(memory_space=pltpu.SMEM)
VMEM = pl.BlockSpec(memory_space=pltpu.VMEM)
ANY = pl.BlockSpec(memory_space=pl.ANY)
HBM = pl.BlockSpec(memory_space=pltpu.HBM)


def cost(flops, moved_bytes):
    return pl.CostEstimate(flops=flops, bytes_accessed=moved_bytes, transcendentals=0)


def shape(dims, kind=BF16):
    return jax.ShapeDtypeStruct(dims, kind)


def limit(mebibytes):
    return pltpu.CompilerParams(vmem_limit_bytes=mebibytes * 1024 * 1024)


def moved(value, target):
    return lax.ppermute(value, "fsdp", [(i, target(i)) for i in range(N_FSDP)])


def to_core(i):
    return i ^ 1


def to_y(i):
    return i ^ 2


def to_next_x(i):
    return (i + 4) % N_FSDP


def to_prev_x(i):
    return (i - 4) % N_FSDP


together = lax.optimization_barrier


def pack_kernel(*refs):
    given, out, held, sems = refs[:4], refs[4], refs[5:9], refs[9]
    copies = [pltpu.make_async_copy(w, h, sems.at[i]) for i, (w, h) in enumerate(zip(given, held))]
    for copy in copies:
        copy.start()
    row = 0
    for copy, ref in zip(copies, held):
        copy.wait()
        rows, cols = ref.shape
        for p in range(cols // HEAD):
            out[row : row + rows] = ref[:, HEAD * p : HEAD * (p + 1)]
            row += rows


def pack(*weights):
    return pl.pallas_call(
        pack_kernel,
        out_shape=shape((PACKED, HEAD)),
        in_specs=[HBM] * 4,
        out_specs=VMEM,
        scratch_shapes=[pltpu.VMEM(w.shape, BF16) for w in weights] + [pltpu.SemaphoreType.DMA((4,))],
        compiler_params=limit(60),
        cost_estimate=cost(0, 4_000_000),
        name="pack",
    )(*weights)


QKV_PART = QKV_PANELS * QKV_ROWS

SLOTS = [(0, 0), (3, 0), (0, 1), (1, 0), (2, 0), (3, 1), (1, 1), (2, 1)]
SLOT_ROWS = 2 * QKV_ROWS
OWN_EARLY, PEER_EARLY = 4, 3


def rms(values, gain):
    mean = jnp.sum(values * values, -1, keepdims=True) * (1.0 / D)
    return values * lax.rsqrt(mean + EPSILON) * gain


def chip_index(position, dx, dy):
    x = position // 4
    y = (position // 2) % 2
    return ((x + dx) % 4) * 2 + (y if dy == 0 else 1 - y)


def device_index(position, dx, dy, dc):
    core = position % 2
    return chip_index(position, dx, dy) * 2 + (core if dc == 0 else 1 - core)


def load_qkv(slots, refs, wqkv, sem):
    for slot, sources in enumerate(slots):
        for dc, (piece, row) in enumerate(sources):
            panels = refs[piece].at[pl.ds(row, QKV_PART)].reshape(QKV_PANELS, QKV_ROWS, HEAD)
            to = pl.ds(SLOT_ROWS * slot + QKV_ROWS * dc, QKV_ROWS)
            pltpu.make_async_copy(panels, wqkv.at[:, to], sem).start()


def load_out(position, slots, refs, wo, sem):
    for (dx, dy), sources in zip(SLOTS, slots):
        for dc, (piece, row) in enumerate(sources):
            rows = pl.ds(row + QKV_PART, O_PANELS * O_ROWS)
            panels = refs[piece].at[rows].reshape(O_PANELS, O_ROWS, HEAD)
            owner = device_index(position, dx, dy, dc)
            to = pl.ds(pl.multiple_of(owner * O_ROWS, 16), O_ROWS)
            pltpu.make_async_copy(panels, wo.at[:, to], sem).start()


def wait_for(ref, sem):
    pltpu.make_async_copy(ref, ref, sem).wait()


def causal_mask():
    row = lax.broadcasted_iota(jnp.int32, (SEQ, SEQ), 0)
    col = lax.broadcasted_iota(jnp.int32, (SEQ, SEQ), 1)
    return row >= col


def nt(a, b):
    return lax.dot_general(a, b, (((1,), (1,)), ((), ())), preferred_element_type=F32)


def tn(a, b):
    return lax.dot_general(a, b, (((0,), (0,)), ((), ())), preferred_element_type=F32)


def nn(a, b):
    return jnp.dot(a, b, preferred_element_type=F32)


def probabilities(query, key, causal):
    capped = jnp.tanh(nt(query, key) * (1.0 / (math.sqrt(HEAD) * ATTN_CAP)))
    scores = jnp.where(causal, ATTN_CAP * capped, MASKED)
    top = jnp.max(scores, -1, keepdims=True)
    weights = jnp.where(causal, jnp.exp(scores - top), 0.0)
    return weights / jnp.sum(weights, -1, keepdims=True), capped


def prepare_kernel(pos_ref, x_ref, gains_ref, *refs):
    parts, (n_mine, n_send, turned, ordered) = refs[:4], refs[4:]
    normed = rms(x_ref[...].astype(F32), gains_ref[0:1, :]).astype(BF16)
    turned[...] = normed.T

    def rows_of(device):
        return turned[pl.ds(pl.multiple_of(device * QKV_ROWS, 16), QKV_ROWS)]

    position = pos_ref[0]
    for slot, (dx, dy) in enumerate(SLOTS):
        for dc in range(2):
            to = SLOT_ROWS * slot + QKV_ROWS * dc
            ordered[to : to + QKV_ROWS] = rows_of(device_index(position, dx, dy, dc))
    for split, early, late in ((OWN_EARLY, *parts[:2]), (PEER_EARLY, *parts[2:])):
        early[...] = ordered[0 : SLOT_ROWS * split].T
        late[...] = ordered[SLOT_ROWS * split :].T
    core = position % 2
    for chip in range(8):
        to = slice(QKV_ROWS * chip, QKV_ROWS * (chip + 1))
        n_mine[to] = rows_of(2 * chip + core)
        n_send[to] = rows_of(2 * chip + 1 - core)


def early_kernel(slots, normed, *refs):
    pieces, (acc, wqkv, sem) = refs[:-3], refs[-3:]
    load_qkv(slots, pieces, wqkv, sem)
    wait_for(wqkv, sem)

    def one_panel(p, carry):
        acc[p] = nn(normed[...], wqkv[p])
        return carry

    lax.fori_loop(0, QKV_PANELS, one_panel, 0)


def layer(position, early, slots, x_ref, gains_ref, head_ref, normed, acc, pieces, qkv, context, hidden, wqkv, wo, sems):
    load_qkv(slots[early:], pieces, wqkv, sems.at[0])
    load_out(position, slots, pieces, wo, sems.at[1])
    wait_for(wqkv, sems.at[0])

    def one_panel(p, carry):
        qkv[p] = (acc[p] + nn(normed[...], wqkv[p])).astype(BF16)
        return carry

    lax.fori_loop(0, QKV_PANELS, one_panel, 0)
    causal = causal_mask()
    for h in range(HQ):
        group = h // (HQ // HK)
        probs, _ = probabilities(qkv[h], qkv[HQ + group], causal)
        context[:, HEAD * h : HEAD * (h + 1)] = nn(
            probs.astype(BF16), qkv[HQ + HK + group]
        ).astype(BF16)
    wait_for(wo, sems.at[1])

    def one_out(p, carry):
        cols = pl.ds(pl.multiple_of(p * HEAD, HEAD), HEAD)
        hidden[:, cols] = x_ref[:, cols].astype(F32) + nn(context[...], wo[p])
        return carry

    lax.fori_loop(0, O_PANELS, one_out, 0)
    final = rms(hidden[...], gains_ref[1:2, :]).astype(BF16)
    logits = LABEL_CAP * jnp.tanh(nn(final, head_ref[...]) * (1.0 / LABEL_CAP))
    return logits, logits - jnp.log(jnp.sum(jnp.exp(logits), -1, keepdims=True))


def own_kernel(slots, pos_ref, x_ref, gains_ref, head_ref, normed, acc, *refs):
    pieces, refs = refs[:-14], refs[-14:]
    c_mine, c_send, qkv_out, hidden_out, logits, wo_out, qkv, hidden, context, turned, wqkv, wo, sems, out_sems = refs
    position = pos_ref[0]
    logits[...], _ = layer(
        *(position, OWN_EARLY, slots, x_ref, gains_ref, head_ref, normed, acc, pieces),
        *(qkv, context, hidden, wqkv, wo, sems),
    )
    copies = [
        pltpu.make_async_copy(wo, wo_out, out_sems.at[0]),
        pltpu.make_async_copy(hidden, hidden_out, out_sems.at[1]),
        pltpu.make_async_copy(qkv, qkv_out, out_sems.at[2]),
    ]
    for copy in copies:
        copy.start()
    turned[...] = context[...].T
    core = position % 2
    for chip in range(8):
        to = slice(O_ROWS * chip, O_ROWS * (chip + 1))
        at = pl.multiple_of((2 * chip + core) * O_ROWS, 16)
        c_mine[to] = turned[pl.ds(at, O_ROWS)]
        at = pl.multiple_of((2 * chip + 1 - core) * O_ROWS, 16)
        c_send[to] = turned[pl.ds(at, O_ROWS)]
    for copy in copies:
        copy.wait()


def peer_kernel(
    slots, pos_ref, x_ref, gains_ref, head_ref, normed, acc, labels_ref, own_logits, own_hidden, *refs
):
    pieces, refs = refs[:-8], refs[-8:]
    loss, dhidden, qkv, context, hidden, wqkv, wo, sems = refs
    _, peer_lp = layer(
        pos_ref[0], PEER_EARLY, slots, x_ref, gains_ref, head_ref, normed, acc, pieces, qkv, context, hidden, wqkv, wo, sems
    )
    logits = own_logits[...]
    own_lp = logits - jnp.log(jnp.sum(jnp.exp(logits), -1, keepdims=True))
    peer = jnp.exp(peer_lp)
    hot = labels_ref[...] == lax.broadcasted_iota(jnp.int32, (SEQ, LABELS), 1)
    picked = jnp.sum(jnp.where(hot, own_lp, 0.0), -1, keepdims=True)
    loss[...] = jnp.sum(peer * (peer_lp - own_lp), -1, keepdims=True) - picked
    d_lp = (jnp.where(hot, 1.0, 0.0) + peer) * (-1.0 / SEQ)
    d_logits = d_lp - jnp.exp(own_lp) * jnp.sum(d_lp, -1, keepdims=True)
    capped = logits * (1.0 / LABEL_CAP)
    d_raw = (d_logits * (1.0 - capped * capped)).astype(BF16)
    d_final = nt(d_raw, head_ref[...]).astype(BF16).astype(F32) * gains_ref[1:2, :]
    own = own_hidden[...]
    scale = lax.rsqrt(jnp.sum(own * own, -1, keepdims=True) * (1.0 / D) + EPSILON)
    along = jnp.sum(d_final * own, -1, keepdims=True) * (1.0 / D)
    dhidden[...] = (d_final * scale - own * (scale * scale * scale * along)).astype(BF16)


def attention_back_kernel(dhidden, wo_panels, qkv, dqkv, wo, sem):
    for p in range(O_PANELS):
        pltpu.make_async_copy(wo_panels.at[p], wo.at[:, pl.ds(HEAD * p, HEAD)], sem).start()
    wait_for(wo, sem)
    causal = causal_mask()
    for group in range(HK):
        key, value = qkv[HQ + group], qkv[HQ + HK + group]
        d_key = jnp.zeros((SEQ, HEAD), F32)
        d_value = jnp.zeros((SEQ, HEAD), F32)
        for h in range(group * (HQ // HK), (group + 1) * (HQ // HK)):
            query = qkv[h]
            probs, capped = probabilities(query, key, causal)
            d_out = nt(dhidden[...], wo[HEAD * h : HEAD * (h + 1), :]).astype(BF16)
            d_value += tn(probs.astype(BF16), d_out)
            d_probs = nt(d_out, value).astype(BF16).astype(F32)
            d_scores = probs * (d_probs - jnp.sum(d_probs * probs, -1, keepdims=True))
            d_raw = (d_scores * (1.0 - capped * capped) * (1.0 / math.sqrt(HEAD))).astype(BF16)
            dqkv[h] = nn(d_raw, key).astype(BF16)
            d_key += tn(d_raw, query)
        dqkv[HQ + group] = d_key.astype(BF16)
        dqkv[HQ + HK + group] = d_value.astype(BF16)


CHIPS = [(0, 0), (1, 0), (2, 0), (3, 0), (0, 1), (1, 1), (2, 1), (3, 1)]


def block_outs(outs):
    return [[o] for o in outs[:6]] + [list(outs[6:9])] + [[outs[9]]]


def hand_out(position, outs, whole_blocks):
    for parts, (dx, dy) in zip(block_outs(outs), CHIPS):
        at = chip_index(position, dx, dy)
        row = 0
        for part in parts:
            part[...] = whole_blocks[at, row : row + part.shape[0]]
            row += part.shape[0]


def out_grad_kernel(pos_ref, mine, other, d_mine, d_other, *refs):
    outs, (lhs, rhs, blocks) = refs[:10], refs[10:]
    lhs[:, 0:SEQ], lhs[:, SEQ : 2 * SEQ] = mine[...], other[...]
    rhs[0:SEQ], rhs[SEQ : 2 * SEQ] = d_mine[...], d_other[...]

    def one_panel(p, carry):
        cols = pl.ds(pl.multiple_of(p * HEAD, HEAD), HEAD)
        rows = pl.ds(pl.multiple_of(p * O_ROWS, 16), O_ROWS)
        total = nn(lhs[...], rhs[:, cols]).astype(BF16)
        for chip in range(8):
            blocks[chip, rows] = total[O_ROWS * chip : O_ROWS * (chip + 1)]
        return carry

    lax.fori_loop(0, O_PANELS, one_panel, 0)
    hand_out(pos_ref[0], outs, blocks)


def qkv_grad_kernel(pos_ref, mine, other, d_mine, d_other, *refs):
    outs, (lhs, rhs, blocks) = refs[:10], refs[10:]
    lhs[:, 0:SEQ], lhs[:, SEQ : 2 * SEQ] = mine[...], other[...]
    rhs[:, 0:SEQ], rhs[:, SEQ : 2 * SEQ] = d_mine[...], d_other[...]

    def one_panel(p, carry):
        rows = pl.ds(pl.multiple_of(p * QKV_ROWS, 16), QKV_ROWS)
        total = nn(lhs[...], rhs[p]).astype(BF16)
        for chip in range(8):
            blocks[chip, rows] = total[QKV_ROWS * chip : QKV_ROWS * (chip + 1)]
        return carry

    lax.fori_loop(0, QKV_PANELS, one_panel, 0)
    hand_out(pos_ref[0], outs, blocks)


def prepare(position, x, gains):
    return pl.pallas_call(
        prepare_kernel,
        out_shape=[
            shape((SEQ, SLOT_ROWS * count))
            for count in (OWN_EARLY, 8 - OWN_EARLY, PEER_EARLY, 8 - PEER_EARLY)
        ]
        + [shape((D // 2, SEQ))] * 2,
        in_specs=[SMEM, VMEM, VMEM],
        out_specs=[VMEM] * 6,
        scratch_shapes=[pltpu.VMEM((D, SEQ), BF16)] * 2,
        compiler_params=limit(20),
        cost_estimate=cost(10_000_000, 10_000_000),
        name="prepare",
    )(position, x, gains)


def some_wqkv(count):
    return pltpu.VMEM((QKV_PANELS, SLOT_ROWS * count, HEAD), BF16)


def early_pass(normed, arrays, slots):
    return pl.pallas_call(
        functools.partial(early_kernel, slots),
        out_shape=shape((QKV_PANELS, SEQ, HEAD), F32),
        in_specs=[VMEM] + [ANY] * len(arrays),
        out_specs=VMEM,
        scratch_shapes=[some_wqkv(len(slots)), pltpu.SemaphoreType.DMA],
        compiler_params=limit(14),
        cost_estimate=cost(1_200_000_000, 20_000_000),
        name="early_pass",
    )(normed, *arrays)


def own_pass(position, x, gains, head, normed, acc, arrays, slots):
    return pl.pallas_call(
        functools.partial(own_kernel, slots),
        out_shape=[
            shape((HQ * HEAD // 2, SEQ)),
            shape((HQ * HEAD // 2, SEQ)),
            shape((QKV_PANELS, SEQ, HEAD)),
            shape((SEQ, D), F32),
            shape((SEQ, LABELS), F32),
            shape((O_PANELS, HQ * HEAD, HEAD)),
        ],
        in_specs=[SMEM] + [VMEM] * 5 + [ANY] * len(arrays),
        out_specs=[VMEM, VMEM, HBM, HBM, VMEM, HBM],
        scratch_shapes=[
            pltpu.VMEM((QKV_PANELS, SEQ, HEAD), BF16),
            pltpu.VMEM((SEQ, D), F32),
            pltpu.VMEM((SEQ, HQ * HEAD), BF16),
            pltpu.VMEM((HQ * HEAD, SEQ), BF16),
            some_wqkv(8 - OWN_EARLY),
            pltpu.VMEM((O_PANELS, HQ * HEAD, HEAD), BF16),
            pltpu.SemaphoreType.DMA((2,)),
            pltpu.SemaphoreType.DMA((3,)),
        ],
        compiler_params=limit(60),
        cost_estimate=cost(3_000_000_000, 30_000_000),
        name="own_pass",
    )(position, x, gains, head, normed, acc, *arrays)


def peer_pass(position, x, gains, head, normed, acc, labels, own_logits, own_hidden, arrays, slots):
    return pl.pallas_call(
        functools.partial(peer_kernel, slots),
        out_shape=[shape((SEQ, 1), F32), shape((SEQ, D))],
        in_specs=[SMEM] + [VMEM] * 8 + [ANY] * len(arrays),
        out_specs=[VMEM] * 2,
        scratch_shapes=[
            pltpu.VMEM((QKV_PANELS, SEQ, HEAD), BF16),
            pltpu.VMEM((SEQ, HQ * HEAD), BF16),
            pltpu.VMEM((SEQ, D), F32),
            some_wqkv(8 - PEER_EARLY),
            pltpu.VMEM((O_PANELS, HQ * HEAD, HEAD), BF16),
            pltpu.SemaphoreType.DMA((2,)),
        ],
        compiler_params=limit(26),
        cost_estimate=cost(3_000_000_000, 30_000_000),
        name="peer_pass",
    )(position, x, gains, head, normed, acc, labels, own_logits, own_hidden, *arrays)


def attention_back(dhidden, wo, qkv):
    return pl.pallas_call(
        attention_back_kernel,
        out_shape=shape((QKV_PANELS, SEQ, HEAD)),
        in_specs=[VMEM, HBM, VMEM],
        out_specs=VMEM,
        scratch_shapes=[pltpu.VMEM((HQ * HEAD, D), BF16), pltpu.SemaphoreType.DMA],
        compiler_params=limit(20),
        cost_estimate=cost(2_000_000_000, 16_000_000),
        name="attention_back",
    )(dhidden, wo, qkv)


def weight_grads(kernel, rows, panels, rhs, position, mine, other, d_mine, d_other, name):
    block = rows * panels
    return pl.pallas_call(
        kernel,
        out_shape=[shape((block, HEAD))] * 6 + [shape((block // 3, HEAD))] * 3 + [shape((block, HEAD))],
        in_specs=[SMEM] + [VMEM] * 4,
        out_specs=[VMEM] * 10,
        scratch_shapes=[
            pltpu.VMEM((8 * rows, 2 * SEQ), BF16),
            pltpu.VMEM(rhs, BF16),
            pltpu.VMEM((8, block, HEAD), BF16),
        ],
        compiler_params=limit(28),
        cost_estimate=cost(2 * 8 * rows * 2 * SEQ * panels * HEAD, 10_000_000),
        name=name,
    )(position, mine, other, d_mine, d_other)


def third_added_kernel(a2, o3, o1, in_a, in_b, in_c, a2_out, o3_out, o1_out):
    t = in_a.shape[0]
    for third, (value, more, out) in enumerate(
        ((a2, in_a, a2_out), (o3, in_b, o3_out), (o1, in_c, o1_out))
    ):
        for part in range(3):
            rows = slice(t * part, t * (part + 1))
            if part == third:
                out[rows] = (value[rows].astype(F32) + more[...].astype(F32)).astype(BF16)
            else:
                out[rows] = value[rows]


def next_added_kernel(a1, o0, in_x, in_y, in_o0, a1_out, o0_out):
    total = a1[...].astype(F32) + in_x[...].astype(F32) + in_y[...].astype(F32)
    a1_out[...] = total.astype(BF16)
    o0_out[...] = (o0[...].astype(F32) + in_o0[...].astype(F32)).astype(BF16)


def summed_kernel(rows, *refs):
    parts, outs = refs[:4], refs[4:]
    row = 0
    for out in outs:
        for p in range(out.shape[1] // HEAD):
            at = slice(row, row + rows)
            total = parts[0][at].astype(F32)
            for part in parts[1:]:
                total += part[at].astype(F32)
            out[:, HEAD * p : HEAD * (p + 1)] = total
            row += rows


def elementwise(kernel, outs, name, *values):
    return pl.pallas_call(
        kernel,
        out_shape=outs,
        in_specs=[VMEM] * len(values),
        out_specs=[VMEM] * len(outs),
        compiler_params=limit(12),
        cost_estimate=cost(1_000_000, 4_000_000),
        name=name,
    )(*values)


def reduce_first(blocks):
    return moved(blocks[6], to_y), moved(blocks[7], to_prev_x), moved(blocks[8], to_next_x)


def add_thirds(blocks, incoming):
    a2, o3, o1 = blocks[2], blocks[9], blocks[5]
    outs = [shape(a2.shape)] * 3
    return elementwise(third_added_kernel, outs, "add_thirds", a2, o3, o1, *incoming)


def reduce_rest(blocks, added, rows, widths):
    s0, a1, _, a3, o0, *_ = blocks
    a2, o3, o1 = added
    one = shape(s0.shape)
    in_x, in_o0, in_y = together((moved(a2, to_next_x), moved(o3, to_prev_x), moved(o1, to_y)))
    a1, o0 = elementwise(next_added_kernel, [one] * 2, "add_next", a1, o0, in_x, in_y, in_o0)
    last = together((moved(a1, to_next_x), moved(a3, to_prev_x), moved(o0, to_y)))
    outs = [shape((rows, width), F32) for width in widths]
    return elementwise(functools.partial(summed_kernel, rows), outs, "add_last", s0, *last)


def body(
    activations,
    labels,
    own_q,
    own_k,
    own_v,
    own_o,
    peer_q,
    peer_k,
    peer_v,
    peer_o,
    norm_gains,
    label_head,
):
    me = lax.axis_index("fsdp")
    position = me.astype(jnp.int32).reshape(1)
    x = activations[0, 0]
    replicas = lax.axis_size("replica")

    own = pack(own_q[0], own_k[0], own_v[0], own_o[0])
    peer = pack(peer_q[0], peer_k[0], peer_v[0], peer_o[0])

    a1, a3 = moved(own, to_prev_x), moved(own, to_next_x)
    peer = lax.ppermute(peer, "replica", [(i, (i + 1) % replicas) for i in range(replicas)])
    prepared = prepare(position, x, norm_gains)
    a1, a3, peer, own, prepared = together((a1, a3, peer, own, prepared))
    n_early, n_late, n_peer_early, n_peer_late, n_mine, n_send = prepared

    y0, a2, p_a3 = moved(own, to_y), moved(a1, to_prev_x), moved(peer, to_next_x)
    n_other = moved(n_send, to_core)
    joined = jnp.concatenate([own, a3, a1], 0)
    y0, a2, p_a3, joined, n_other = together((y0, a2, p_a3, joined, n_other))

    p_y0, o3, o1 = moved(peer, to_y), moved(y0, to_next_x), moved(y0, to_prev_x)
    swap_first, swap_a2 = moved(joined, to_core), moved(a2, to_core)
    p_y0, o3, o1, swap_first, swap_a2 = together((p_y0, o3, o1, swap_first, swap_a2))

    o2, p_a1, p_o3 = moved(a2, to_y), moved(peer, to_prev_x), moved(p_y0, to_next_x)
    swap_y0, swap_o3 = moved(y0, to_core), moved(o3, to_core)

    def all_of(piece, at=0):
        return (piece, at)

    own_slots = [
        (all_of(0), all_of(4, 0)),
        (all_of(1), all_of(4, PACKED)),
        (all_of(2), all_of(5)),
        (all_of(3), all_of(4, 2 * PACKED)),
        (all_of(6), all_of(10)),
        (all_of(7), all_of(11)),
        (all_of(8), all_of(12)),
        (all_of(9), all_of(13)),
    ]
    acc = early_pass(n_early, [own, a3, y0, a1, swap_first, swap_y0], own_slots[:OWN_EARLY])
    joined = jnp.concatenate([peer, p_a3, p_y0], 0)
    o2, p_a1, p_o3, swap_o3, joined, acc = together((o2, p_a1, p_o3, swap_o3, joined, acc))

    p_o1, p_a2, p_o2 = moved(p_a1, to_y), moved(p_a1, to_prev_x), moved(p_o3, to_next_x)
    swap_o1, swap_o2 = moved(o1, to_core), moved(o2, to_core)
    p_swap_first = moved(joined, to_core)
    c_mine, c_send, qkv, hidden, logits, wo = own_pass(
        position,
        x,
        norm_gains,
        label_head,
        n_late,
        acc,
        [own, a3, y0, a1, swap_first, swap_y0, a2, o3, o1, o2, swap_a2, swap_o3, swap_o1, swap_o2],
        own_slots,
    )
    p_o1, p_a2, p_o2, p_swap_first, c_send, hidden = together(
        (p_o1, p_a2, p_o2, p_swap_first, c_send, hidden)
    )

    late = [p_a1, p_a2, p_o3, p_o1, p_o2]
    swap_late = [moved(piece, to_core) for piece in late]
    c_other = moved(c_send, to_core)
    peer_slots = [(all_of(i), all_of(3, PACKED * i)) for i in range(PEER_EARLY)]
    p_acc = early_pass(n_peer_early, [peer, p_a3, p_y0, p_swap_first], peer_slots)
    peer_slots = peer_slots + [(all_of(4 + i), all_of(9 + i)) for i in range(8 - PEER_EARLY)]
    loss, dhidden = peer_pass(
        position,
        x,
        norm_gains,
        label_head,
        n_peer_late,
        p_acc,
        labels[0, 0].reshape(SEQ, 1),
        logits,
        hidden,
        [peer, p_a3, p_y0, p_swap_first, *late, *swap_late],
        peer_slots,
    )
    dhidden, c_other = together((dhidden, c_other))
    d_other = moved(dhidden, to_core)
    dqkv = attention_back(dhidden, wo, qkv)
    dqkv_other = moved(dqkv, to_core)
    out_blocks = weight_grads(
        out_grad_kernel,
        *(O_ROWS, O_PANELS, (2 * SEQ, D)),
        *(position, c_mine, c_other, dhidden, d_other, "out_grads"),
    )
    dqkv, dqkv_other, *out_blocks = together((dqkv, dqkv_other, *out_blocks))
    qkv_blocks = weight_grads(
        qkv_grad_kernel,
        *(QKV_ROWS, QKV_PANELS, (QKV_PANELS, 2 * SEQ, HEAD)),
        *(position, n_mine, n_other, dqkv, dqkv_other, "qkv_grads"),
    )
    in_a, in_b, in_c, *qkv_blocks = together((*reduce_first(out_blocks), *qkv_blocks))
    added, qkv_blocks = together((add_thirds(out_blocks, (in_a, in_b, in_c)), qkv_blocks))
    (grad_out,) = reduce_rest(out_blocks, added, O_ROWS, [D])
    added = add_thirds(qkv_blocks, together(reduce_first(qkv_blocks)))
    grads = reduce_rest(qkv_blocks, added, QKV_ROWS, [HQ * HEAD, HK * HEAD, HK * HEAD])
    return (loss.reshape(1, 1, SEQ), *[grad[None] for grad in grads], grad_out[None])


def solution(mesh):
    weights = P("replica", "fsdp", None)
    return jax.shard_map(
        body,
        mesh=mesh,
        in_specs=(P("replica", "fsdp", None, None), weights, *([weights] * 8), P(), P()),
        out_specs=(weights,) * 5,
        check_vma=False,
    )
```

```python
import functools
import math

import jax
import jax.numpy as jnp
from jax import lax
from jax.experimental import pallas as pl
from jax.experimental.pallas import tpu as pltpu
from jax.sharding import PartitionSpec as P

SEQ, D, HEAD, HQ, HK, LABELS = 256, 2304, 256, 4, 2, 256
QKV_PANELS, O_PANELS = 8, 9
QKV_ROWS, O_ROWS = 144, 64
THIRD = 576
PACKED = 3 * THIRD
EPSILON = 1e-06
ATTN_CAP = 50.0
LABEL_CAP = 30.0
MASKED = -1e30
F32, BF16 = jnp.float32, jnp.bfloat16

N_FSDP = 16


SMEM = pl.BlockSpec(memory_space=pltpu.SMEM)
VMEM = pl.BlockSpec(memory_space=pltpu.VMEM)
ANY = pl.BlockSpec(memory_space=pl.ANY)
HBM = pl.BlockSpec(memory_space=pltpu.HBM)


def cost(flops, moved_bytes):
    return pl.CostEstimate(flops=flops, bytes_accessed=moved_bytes, transcendentals=0)


def shape(dims, kind=BF16):
    return jax.ShapeDtypeStruct(dims, kind)


def limit(mebibytes):
    return pltpu.CompilerParams(vmem_limit_bytes=mebibytes * 1024 * 1024)


def moved(value, target):
    return lax.ppermute(value, "fsdp", [(i, target(i)) for i in range(N_FSDP)])


def to_core(i):
    return i ^ 1


def to_y(i):
    return i ^ 2


def to_next_x(i):
    return (i + 4) % N_FSDP


def to_prev_x(i):
    return (i - 4) % N_FSDP


together = lax.optimization_barrier


def pack_kernel(*refs):
    given, outs, held, sems = refs[:8], refs[8:10], refs[10:18], refs[18]
    copies = [pltpu.make_async_copy(w, h, sems.at[i]) for i, (w, h) in enumerate(zip(given, held))]
    for copy in copies:
        copy.start()
    for i, (copy, ref) in enumerate(zip(copies, held)):
        row = 0 if i % 4 == 0 else row
        copy.wait()
        rows, cols = ref.shape
        for p in range(cols // HEAD):
            outs[i // 4][row : row + rows] = ref[:, HEAD * p : HEAD * (p + 1)]
            row += rows


def pack(*weights):
    return pl.pallas_call(
        pack_kernel,
        out_shape=[shape((PACKED, HEAD))] * 2,
        in_specs=[HBM] * 8,
        out_specs=[VMEM] * 2,
        scratch_shapes=[pltpu.VMEM(w.shape, BF16) for w in weights] + [pltpu.SemaphoreType.DMA((8,))],
        compiler_params=limit(60),
        cost_estimate=cost(0, 8_000_000),
        name="pack",
    )(*weights)


QKV_PART = QKV_PANELS * QKV_ROWS

SLOTS = [(0, 0), (3, 0), (0, 1), (1, 0), (3, 1), (2, 0), (1, 1), (2, 1)]
SLOT_ROWS = 2 * QKV_ROWS
EARLY = 4


def rms(values, gain):
    mean = jnp.sum(values * values, -1, keepdims=True) * (1.0 / D)
    return values * lax.rsqrt(mean + EPSILON) * gain


CHIPS = [(0, 0), (1, 0), (2, 0), (3, 0), (0, 1), (1, 1), (2, 1), (3, 1)]


def chip_index(position, dx, dy):
    x = position // 4
    y = (position // 2) % 2
    return ((x + dx) % 4) * 2 + (y if dy == 0 else 1 - y)


def device_index(position, dx, dy, dc):
    core = position % 2
    return chip_index(position, dx, dy) * 2 + (core if dc == 0 else 1 - core)


def load_qkv(slots, refs, wqkv, sem):
    for slot, sources in enumerate(slots):
        for dc, (piece, row) in enumerate(sources):
            panels = refs[piece].at[pl.ds(row, QKV_PART)].reshape(QKV_PANELS, QKV_ROWS, HEAD)
            to = pl.ds(SLOT_ROWS * slot + QKV_ROWS * dc, QKV_ROWS)
            pltpu.make_async_copy(panels, wqkv.at[:, to], sem).start()


def load_out(position, slots, refs, wo, sem):
    for (dx, dy), sources in zip(SLOTS, slots):
        for dc, (piece, row) in enumerate(sources):
            rows = pl.ds(row + QKV_PART, O_PANELS * O_ROWS)
            panels = refs[piece].at[rows].reshape(O_PANELS, O_ROWS, HEAD)
            owner = device_index(position, dx, dy, dc)
            to = pl.ds(pl.multiple_of(owner * O_ROWS, 16), O_ROWS)
            pltpu.make_async_copy(panels, wo.at[:, to], sem).start()


def wait_for(ref, sem):
    pltpu.make_async_copy(ref, ref, sem).wait()


def causal_mask():
    row = lax.broadcasted_iota(jnp.int32, (SEQ, SEQ), 0)
    col = lax.broadcasted_iota(jnp.int32, (SEQ, SEQ), 1)
    return row >= col


def nt(a, b):
    return lax.dot_general(a, b, (((1,), (1,)), ((), ())), preferred_element_type=F32)


def tn(a, b):
    return lax.dot_general(a, b, (((0,), (0,)), ((), ())), preferred_element_type=F32)


def nn(a, b):
    return jnp.dot(a, b, preferred_element_type=F32)


def probabilities(query, key, causal):
    capped = jnp.tanh(nt(query, key) * (1.0 / (math.sqrt(HEAD) * ATTN_CAP)))
    scores = jnp.where(causal, ATTN_CAP * capped, MASKED)
    top = jnp.max(scores, -1, keepdims=True)
    weights = jnp.where(causal, jnp.exp(scores - top), 0.0)
    return weights / jnp.sum(weights, -1, keepdims=True), capped


def prepare_kernel(pos_ref, x_ref, gains_ref, *refs):
    early, late, n_mine, n_send, turned, ordered = refs
    normed = rms(x_ref[...].astype(F32), gains_ref[0:1, :]).astype(BF16)
    turned[...] = normed.T

    def rows_of(device):
        return turned[pl.ds(pl.multiple_of(device * QKV_ROWS, 16), QKV_ROWS)]

    position = pos_ref[0]
    for slot, (dx, dy) in enumerate(SLOTS):
        for dc in range(2):
            to = SLOT_ROWS * slot + QKV_ROWS * dc
            ordered[to : to + QKV_ROWS] = rows_of(device_index(position, dx, dy, dc))
    early[...] = ordered[0 : SLOT_ROWS * EARLY].T
    late[...] = ordered[SLOT_ROWS * EARLY :].T
    for chip, (dx, dy) in enumerate(CHIPS):
        to = slice(QKV_ROWS * chip, QKV_ROWS * (chip + 1))
        n_mine[to] = rows_of(device_index(position, dx, dy, 0))
        n_send[to] = rows_of(device_index(position, dx, dy, 1))


def early_kernel(slots, normed, *refs):
    pieces, (acc, wqkv, sem) = refs[:-3], refs[-3:]
    load_qkv(slots, pieces, wqkv, sem)
    wait_for(wqkv, sem)

    def one_panel(p, carry):
        acc[p] = nn(normed[...], wqkv[p])
        return carry

    lax.fori_loop(0, QKV_PANELS, one_panel, 0)


def layer(position, early, slots, x_ref, gains_ref, head_ref, normed, acc, pieces, qkv, context, hidden, wqkv, wo, sems, reached=lambda stage: None):
    load_qkv(slots[early:], pieces, wqkv, sems.at[0])
    load_out(position, slots, pieces, wo, sems.at[1])
    reached("loads")
    wait_for(wqkv, sems.at[0])

    def one_panel(p, carry):
        qkv[p] = (acc[p] + nn(normed[...], wqkv[p])).astype(BF16)
        return carry

    lax.fori_loop(0, QKV_PANELS, one_panel, 0)
    reached("qkv")
    causal = causal_mask()
    for h in range(HQ):
        group = h // (HQ // HK)
        probs, _ = probabilities(qkv[h], qkv[HQ + group], causal)
        context[:, HEAD * h : HEAD * (h + 1)] = nn(
            probs.astype(BF16), qkv[HQ + HK + group]
        ).astype(BF16)
    wait_for(wo, sems.at[1])
    reached("out")

    def one_out(p, carry):
        cols = pl.ds(pl.multiple_of(p * HEAD, HEAD), HEAD)
        hidden[:, cols] = x_ref[:, cols].astype(F32) + nn(context[...], wo[p])
        return carry

    lax.fori_loop(0, O_PANELS, one_out, 0)
    reached("hidden")
    final = rms(hidden[...], gains_ref[1:2, :]).astype(BF16)
    logits = LABEL_CAP * jnp.tanh(nn(final, head_ref[...]) * (1.0 / LABEL_CAP))
    return logits, logits - jnp.log(jnp.sum(jnp.exp(logits), -1, keepdims=True))


def own_kernel(slots, pos_ref, x_ref, gains_ref, head_ref, normed, acc, *refs):
    pieces, refs = refs[:-18], refs[-18:]
    c_mine, c_send, qkv_out, hidden_out, logits, wo_out = refs[:6]
    x, head, late, sums, qkv, hidden, context, turned, wqkv, wo, sems, more_sems = refs[6:]
    position = pos_ref[0]

    def copy(source, target, i):
        return pltpu.make_async_copy(source, target, more_sems.at[i])

    reads = [copy(normed, late, 0), copy(acc, sums, 1), copy(x_ref, x, 2), copy(head_ref, head, 3)]
    writes = [copy(qkv, qkv_out, 4), copy(wo, wo_out, 5), copy(hidden, hidden_out, 6)]

    def reached(stage):
        if stage == "loads":
            for read in reads:
                read.start()
            reads[0].wait()
            reads[1].wait()
        if stage == "qkv":
            writes[0].start()
        if stage == "out":
            writes[1].start()
            reads[2].wait()
        if stage == "hidden":
            writes[2].start()
            reads[3].wait()

    logits[...], _ = layer(
        *(position, EARLY, slots, x, gains_ref, head, late, sums, pieces),
        *(qkv, context, hidden, wqkv, wo, sems, reached),
    )
    turned[...] = context[...].T
    for chip, (dx, dy) in enumerate(CHIPS):
        to = slice(O_ROWS * chip, O_ROWS * (chip + 1))
        for dc, out in ((0, c_mine), (1, c_send)):
            at = pl.multiple_of(device_index(position, dx, dy, dc) * O_ROWS, 16)
            out[to] = turned[pl.ds(at, O_ROWS)]
    for write in writes:
        write.wait()


def peer_kernel(
    slots, pos_ref, x_ref, gains_ref, head_ref, normed, acc, labels_ref, own_logits, own_hidden, *refs
):
    pieces, refs = refs[:-8], refs[-8:]
    loss, dhidden, qkv, context, hidden, wqkv, wo, sems = refs
    _, peer_lp = layer(
        pos_ref[0], EARLY, slots, x_ref, gains_ref, head_ref, normed, acc, pieces, qkv, context, hidden, wqkv, wo, sems
    )
    logits = own_logits[...]
    own_lp = logits - jnp.log(jnp.sum(jnp.exp(logits), -1, keepdims=True))
    peer = jnp.exp(peer_lp)
    hot = labels_ref[...] == lax.broadcasted_iota(jnp.int32, (SEQ, LABELS), 1)
    picked = jnp.sum(jnp.where(hot, own_lp, 0.0), -1, keepdims=True)
    loss[...] = jnp.sum(peer * (peer_lp - own_lp), -1, keepdims=True) - picked
    d_lp = (jnp.where(hot, 1.0, 0.0) + peer) * (-1.0 / SEQ)
    d_logits = d_lp - jnp.exp(own_lp) * jnp.sum(d_lp, -1, keepdims=True)
    capped = logits * (1.0 / LABEL_CAP)
    d_raw = (d_logits * (1.0 - capped * capped)).astype(BF16)
    d_final = nt(d_raw, head_ref[...]).astype(BF16).astype(F32) * gains_ref[1:2, :]
    own = own_hidden[...]
    scale = lax.rsqrt(jnp.sum(own * own, -1, keepdims=True) * (1.0 / D) + EPSILON)
    along = jnp.sum(d_final * own, -1, keepdims=True) * (1.0 / D)
    dhidden[...] = (d_final * scale - own * (scale * scale * scale * along)).astype(BF16)


def attention_back_kernel(dhidden, wo_panels, qkv, dqkv, wo, probs, capped, sem):
    for p in range(O_PANELS):
        pltpu.make_async_copy(wo_panels.at[p], wo.at[:, pl.ds(HEAD * p, HEAD)], sem).start()
    causal = causal_mask()
    for h in range(HQ):
        probs[h], capped[h] = probabilities(qkv[h], qkv[HQ + h // (HQ // HK)], causal)
    wait_for(wo, sem)
    for group in range(HK):
        key, value = qkv[HQ + group], qkv[HQ + HK + group]
        d_key = jnp.zeros((SEQ, HEAD), F32)
        d_value = jnp.zeros((SEQ, HEAD), F32)
        for h in range(group * (HQ // HK), (group + 1) * (HQ // HK)):
            d_out = nt(dhidden[...], wo[HEAD * h : HEAD * (h + 1), :]).astype(BF16)
            d_value += tn(probs[h].astype(BF16), d_out)
            d_probs = nt(d_out, value).astype(BF16).astype(F32)
            d_scores = probs[h] * (d_probs - jnp.sum(d_probs * probs[h], -1, keepdims=True))
            slope = (1.0 - capped[h] * capped[h]) * (1.0 / math.sqrt(HEAD))
            d_raw = (d_scores * slope).astype(BF16)
            dqkv[h] = nn(d_raw, key).astype(BF16)
            d_key += tn(d_raw, qkv[h])
        dqkv[HQ + group] = d_key.astype(BF16)
        dqkv[HQ + HK + group] = d_value.astype(BF16)


def store(outs, split, panel, total):
    rows = total.shape[0] // 8
    to = pl.ds(pl.multiple_of(panel * rows, 16), rows)
    for chip, out in enumerate((*outs[:6], split, outs[9])):
        out[to] = total[rows * chip : rows * (chip + 1)]


def hand_out(outs, split):
    for third, out in enumerate(outs[6:9]):
        rows = out.shape[0]
        out[...] = split[rows * third : rows * (third + 1)]


def out_grad_kernel(mine, other, d_mine, d_other, *refs):
    outs, (lhs, rhs, split) = refs[:10], refs[10:]
    lhs[:, 0:SEQ], lhs[:, SEQ : 2 * SEQ] = mine[...], other[...]
    rhs[0:SEQ], rhs[SEQ : 2 * SEQ] = d_mine[...], d_other[...]

    def one_panel(p, carry):
        cols = pl.ds(pl.multiple_of(p * HEAD, HEAD), HEAD)
        store(outs, split, p, nn(lhs[...], rhs[:, cols]).astype(BF16))
        return carry

    lax.fori_loop(0, O_PANELS, one_panel, 0)
    hand_out(outs, split)


def qkv_grad_kernel(mine, other, d_mine, d_other, *refs):
    outs, (lhs, rhs, split) = refs[:10], refs[10:]
    lhs[:, 0:SEQ], lhs[:, SEQ : 2 * SEQ] = mine[...], other[...]
    rhs[:, 0:SEQ], rhs[:, SEQ : 2 * SEQ] = d_mine[...], d_other[...]

    def one_panel(p, carry):
        store(outs, split, p, nn(lhs[...], rhs[p]).astype(BF16))
        return carry

    lax.fori_loop(0, QKV_PANELS, one_panel, 0)
    hand_out(outs, split)


def prepare(position, x, gains):
    return pl.pallas_call(
        prepare_kernel,
        out_shape=[
            shape((SEQ, SLOT_ROWS * count))
            for count in (EARLY, 8 - EARLY)
        ]
        + [shape((D // 2, SEQ))] * 2,
        in_specs=[SMEM, VMEM, VMEM],
        out_specs=[VMEM] * 4,
        scratch_shapes=[pltpu.VMEM((D, SEQ), BF16)] * 2,
        compiler_params=limit(20),
        cost_estimate=cost(10_000_000, 10_000_000),
        name="prepare",
    )(position, x, gains)


def some_wqkv(count):
    return pltpu.VMEM((QKV_PANELS, SLOT_ROWS * count, HEAD), BF16)


def early_pass(normed, arrays, slots):
    return pl.pallas_call(
        functools.partial(early_kernel, slots),
        out_shape=shape((QKV_PANELS, SEQ, HEAD), F32),
        in_specs=[VMEM] + [ANY] * len(arrays),
        out_specs=VMEM,
        scratch_shapes=[some_wqkv(len(slots)), pltpu.SemaphoreType.DMA],
        compiler_params=limit(14),
        cost_estimate=cost(1_200_000_000, 20_000_000),
        name="early_pass",
    )(normed, *arrays)


def own_pass(position, x, gains, head, normed, acc, arrays, slots):
    return pl.pallas_call(
        functools.partial(own_kernel, slots),
        out_shape=[
            shape((HQ * HEAD // 2, SEQ)),
            shape((HQ * HEAD // 2, SEQ)),
            shape((QKV_PANELS, SEQ, HEAD)),
            shape((SEQ, D), F32),
            shape((SEQ, LABELS), F32),
            shape((O_PANELS, HQ * HEAD, HEAD)),
        ],
        in_specs=[SMEM, ANY, VMEM, ANY, ANY, ANY] + [ANY] * len(arrays),
        out_specs=[VMEM, VMEM, HBM, HBM, VMEM, HBM],
        scratch_shapes=[
            pltpu.VMEM((SEQ, D), BF16),
            pltpu.VMEM((D, LABELS), BF16),
            pltpu.VMEM((SEQ, SLOT_ROWS * (8 - EARLY)), BF16),
            pltpu.VMEM((QKV_PANELS, SEQ, HEAD), F32),
            pltpu.VMEM((QKV_PANELS, SEQ, HEAD), BF16),
            pltpu.VMEM((SEQ, D), F32),
            pltpu.VMEM((SEQ, HQ * HEAD), BF16),
            pltpu.VMEM((HQ * HEAD, SEQ), BF16),
            some_wqkv(8 - EARLY),
            pltpu.VMEM((O_PANELS, HQ * HEAD, HEAD), BF16),
            pltpu.SemaphoreType.DMA((2,)),
            pltpu.SemaphoreType.DMA((7,)),
        ],
        compiler_params=limit(60),
        cost_estimate=cost(3_000_000_000, 30_000_000),
        name="own_pass",
    )(position, x, gains, head, normed, acc, *arrays)


def peer_pass(position, x, gains, head, normed, acc, labels, own_logits, own_hidden, arrays, slots):
    return pl.pallas_call(
        functools.partial(peer_kernel, slots),
        out_shape=[shape((SEQ, 1), F32), shape((SEQ, D))],
        in_specs=[SMEM] + [VMEM] * 8 + [ANY] * len(arrays),
        out_specs=[VMEM] * 2,
        scratch_shapes=[
            pltpu.VMEM((QKV_PANELS, SEQ, HEAD), BF16),
            pltpu.VMEM((SEQ, HQ * HEAD), BF16),
            pltpu.VMEM((SEQ, D), F32),
            some_wqkv(8 - EARLY),
            pltpu.VMEM((O_PANELS, HQ * HEAD, HEAD), BF16),
            pltpu.SemaphoreType.DMA((2,)),
        ],
        compiler_params=limit(26),
        cost_estimate=cost(3_000_000_000, 30_000_000),
        name="peer_pass",
    )(position, x, gains, head, normed, acc, labels, own_logits, own_hidden, *arrays)


def attention_back(dhidden, wo, qkv):
    return pl.pallas_call(
        attention_back_kernel,
        out_shape=shape((QKV_PANELS, SEQ, HEAD)),
        in_specs=[VMEM, HBM, VMEM],
        out_specs=VMEM,
        scratch_shapes=[
            pltpu.VMEM((HQ * HEAD, D), BF16),
            pltpu.VMEM((HQ, SEQ, SEQ), F32),
            pltpu.VMEM((HQ, SEQ, SEQ), F32),
            pltpu.SemaphoreType.DMA,
        ],
        compiler_params=limit(20),
        cost_estimate=cost(2_000_000_000, 16_000_000),
        name="attention_back",
    )(dhidden, wo, qkv)


def weight_grads(kernel, rows, panels, rhs, mine, other, d_mine, d_other, name):
    block = rows * panels
    return pl.pallas_call(
        kernel,
        out_shape=[shape((block, HEAD))] * 6 + [shape((block // 3, HEAD))] * 3 + [shape((block, HEAD))],
        in_specs=[VMEM] * 4,
        out_specs=[VMEM] * 10,
        scratch_shapes=[
            pltpu.VMEM((8 * rows, 2 * SEQ), BF16),
            pltpu.VMEM(rhs, BF16),
            pltpu.VMEM((block, HEAD), BF16),
        ],
        compiler_params=limit(28),
        cost_estimate=cost(2 * 8 * rows * 2 * SEQ * panels * HEAD, 10_000_000),
        name=name,
    )(mine, other, d_mine, d_other)


def third_added_kernel(a2, o3, o1, in_a, in_b, in_c, a2_out, o3_out, o1_out):
    t = in_a.shape[0]
    for third, (value, more, out) in enumerate(
        ((a2, in_a, a2_out), (o3, in_b, o3_out), (o1, in_c, o1_out))
    ):
        for part in range(3):
            rows = slice(t * part, t * (part + 1))
            if part == third:
                out[rows] = (value[rows].astype(F32) + more[...].astype(F32)).astype(BF16)
            else:
                out[rows] = value[rows]


def next_added_kernel(a1, o0, in_x, in_y, in_o0, a1_out, o0_out):
    total = a1[...].astype(F32) + in_x[...].astype(F32) + in_y[...].astype(F32)
    a1_out[...] = total.astype(BF16)
    o0_out[...] = (o0[...].astype(F32) + in_o0[...].astype(F32)).astype(BF16)


def summed_kernel(rows, *refs):
    parts, outs = refs[:4], refs[4:]
    row = 0
    for out in outs:
        for p in range(out.shape[1] // HEAD):
            at = slice(row, row + rows)
            total = parts[0][at].astype(F32)
            for part in parts[1:]:
                total += part[at].astype(F32)
            out[:, HEAD * p : HEAD * (p + 1)] = total
            row += rows


def elementwise(kernel, outs, name, *values):
    return pl.pallas_call(
        kernel,
        out_shape=outs,
        in_specs=[VMEM] * len(values),
        out_specs=[VMEM] * len(outs),
        compiler_params=limit(12),
        cost_estimate=cost(1_000_000, 4_000_000),
        name=name,
    )(*values)


def reduce_first(blocks):
    return moved(blocks[6], to_y), moved(blocks[7], to_prev_x), moved(blocks[8], to_next_x)


def add_thirds(blocks, incoming):
    a2, o3, o1 = blocks[2], blocks[9], blocks[5]
    outs = [shape(a2.shape)] * 3
    return elementwise(third_added_kernel, outs, "add_thirds", a2, o3, o1, *incoming)


def reduce_rest(blocks, added, rows, widths):
    s0, a1, _, a3, o0, *_ = blocks
    a2, o3, o1 = added
    one = shape(s0.shape)
    in_x, in_o0, in_y = together((moved(a2, to_next_x), moved(o3, to_prev_x), moved(o1, to_y)))
    a1, o0 = elementwise(next_added_kernel, [one] * 2, "add_next", a1, o0, in_x, in_y, in_o0)
    last = together((moved(a1, to_next_x), moved(a3, to_prev_x), moved(o0, to_y)))
    outs = [shape((rows, width), F32) for width in widths]
    return elementwise(functools.partial(summed_kernel, rows), outs, "add_last", s0, *last)


def body(
    activations,
    labels,
    own_q,
    own_k,
    own_v,
    own_o,
    peer_q,
    peer_k,
    peer_v,
    peer_o,
    norm_gains,
    label_head,
):
    me = lax.axis_index("fsdp")
    position = me.astype(jnp.int32).reshape(1)
    x = activations[0, 0]
    replicas = lax.axis_size("replica")

    own, peer = pack(
        *(own_q[0], own_k[0], own_v[0], own_o[0]), *(peer_q[0], peer_k[0], peer_v[0], peer_o[0])
    )

    a1, a3 = moved(own, to_prev_x), moved(own, to_next_x)
    peer = lax.ppermute(peer, "replica", [(i, (i + 1) % replicas) for i in range(replicas)])
    s_own = moved(own, to_core)
    *prepared, n_send = prepare(position, x, norm_gains)
    n_other = moved(n_send, to_core)
    column = labels[0, 0].reshape(SEQ, 1)
    a1, a3, own, s_own, n_other, prepared, column = together(
        (a1, a3, own, s_own, n_other, prepared, column)
    )
    n_early, n_late, n_mine = prepared

    y0, a2, p_a3 = moved(own, to_y), moved(a1, to_prev_x), moved(peer, to_next_x)
    s_a1, s_a3 = moved(a1, to_core), moved(a3, to_core)
    y0, a2, p_a3, s_a1, s_a3 = together((y0, a2, p_a3, s_a1, s_a3))

    p_y0, o3, o1 = moved(peer, to_y), moved(y0, to_next_x), moved(y0, to_prev_x)
    s_y0, s_a2 = moved(y0, to_core), moved(a2, to_core)
    p_y0, o3, o1, s_y0, s_a2 = together((p_y0, o3, o1, s_y0, s_a2))

    o2, p_a1, p_o3 = moved(a2, to_y), moved(peer, to_prev_x), moved(p_y0, to_next_x)
    s_o3, s_o1 = moved(o3, to_core), moved(o1, to_core)
    early, s_early = [own, a3, y0, a1], [s_own, s_a3, s_y0, s_a1]
    acc = early_pass(n_early, early + s_early, [((i, 0), (4 + i, 0)) for i in range(4)])
    joined = jnp.concatenate([peer, p_a3, p_y0], 0)
    o2, p_a1, p_o3, s_o3, s_o1, joined, acc = together((o2, p_a1, p_o3, s_o3, s_o1, joined, acc))

    p_o1, p_a2, p_o2 = moved(p_a1, to_y), moved(p_a1, to_prev_x), moved(p_o3, to_next_x)
    s_o2, s_joined = moved(o2, to_core), moved(joined, to_core)
    s_p_a1 = moved(p_a1, to_core)
    c_mine, c_send, qkv, hidden, logits, wo = own_pass(
        position,
        x,
        norm_gains,
        label_head,
        n_late,
        acc,
        early + [o3, a2, o1, o2] + s_early + [s_o3, s_a2, s_o1, s_o2],
        [((i, 0), (8 + i, 0)) for i in range(8)],
    )
    p_o1, p_a2, p_o2, s_joined, s_p_a1, c_send, hidden = together(
        (p_o1, p_a2, p_o2, s_joined, s_p_a1, c_send, hidden)
    )

    late = [p_o3, p_a2, p_o1, p_o2]
    s_late = [moved(piece, to_core) for piece in late]
    c_other = moved(c_send, to_core)
    arrays = [peer, p_a3, p_y0, p_a1, s_joined, s_p_a1]
    slots = [((i, 0), (4, PACKED * i)) for i in range(3)] + [((3, 0), (5, 0))]
    p_acc = early_pass(n_early, arrays, slots)
    loss, dhidden = peer_pass(
        position,
        x,
        norm_gains,
        label_head,
        n_late,
        p_acc,
        column,
        logits,
        hidden,
        arrays + late + s_late,
        slots + [((6 + i, 0), (10 + i, 0)) for i in range(4)],
    )
    dhidden, c_other = together((dhidden, c_other))
    d_other = moved(dhidden, to_core)
    dqkv = attention_back(dhidden, wo, qkv)
    dqkv_other = moved(dqkv, to_core)
    out_blocks = weight_grads(
        out_grad_kernel,
        *(O_ROWS, O_PANELS, (2 * SEQ, D)),
        *(c_mine, c_other, dhidden, d_other, "out_grads"),
    )
    dqkv, dqkv_other, *out_blocks = together((dqkv, dqkv_other, *out_blocks))
    qkv_blocks = weight_grads(
        qkv_grad_kernel,
        *(QKV_ROWS, QKV_PANELS, (QKV_PANELS, 2 * SEQ, HEAD)),
        *(n_mine, n_other, dqkv, dqkv_other, "qkv_grads"),
    )
    in_a, in_b, in_c, *qkv_blocks = together((*reduce_first(out_blocks), *qkv_blocks))
    added = add_thirds(out_blocks, (in_a, in_b, in_c))
    (grad_out,) = reduce_rest(out_blocks, added, O_ROWS, [D])
    added = add_thirds(qkv_blocks, together(reduce_first(qkv_blocks)))
    grads = reduce_rest(qkv_blocks, added, QKV_ROWS, [HQ * HEAD, HK * HEAD, HK * HEAD])
    return (loss.reshape(1, 1, SEQ), *[grad[None] for grad in grads], grad_out[None])


def solution(mesh):
    weights = P("replica", "fsdp", None)
    return jax.shard_map(
        body,
        mesh=mesh,
        in_specs=(P("replica", "fsdp", None, None), weights, *([weights] * 8), P(), P()),
        out_specs=(weights,) * 5,
        check_vma=False,
    )
```

```python
import functools
import math

import jax
import jax.numpy as jnp
from jax import lax
from jax.experimental import pallas as pl
from jax.experimental.pallas import tpu as pltpu
from jax.sharding import PartitionSpec as P

SEQ, D, HEAD, HQ, HK, LABELS = 256, 2304, 256, 4, 2, 256
QKV_PANELS, O_PANELS = 8, 9
QKV_ROWS, O_ROWS = 144, 64
THIRD = 576
PACKED = 3 * THIRD
EPSILON = 1e-06
ATTN_CAP = 50.0
LABEL_CAP = 30.0
MASKED = -1e30
F32, BF16 = jnp.float32, jnp.bfloat16

N_FSDP = 16


SMEM = pl.BlockSpec(memory_space=pltpu.SMEM)
VMEM = pl.BlockSpec(memory_space=pltpu.VMEM)
ANY = pl.BlockSpec(memory_space=pl.ANY)
HBM = pl.BlockSpec(memory_space=pltpu.HBM)


def cost(flops, moved_bytes):
    return pl.CostEstimate(flops=flops, bytes_accessed=moved_bytes, transcendentals=0)


def shape(dims, kind=BF16):
    return jax.ShapeDtypeStruct(dims, kind)


def limit(mebibytes):
    return pltpu.CompilerParams(vmem_limit_bytes=mebibytes * 1024 * 1024)


def moved(value, target):
    return lax.ppermute(value, "fsdp", [(i, target(i)) for i in range(N_FSDP)])


def to_core(i):
    return i ^ 1


def to_y(i):
    return i ^ 2


def to_next_x(i):
    return (i + 4) % N_FSDP


def to_prev_x(i):
    return (i - 4) % N_FSDP


together = lax.optimization_barrier


def pack_kernel(*refs):
    given, outs, held, sems = refs[:8], refs[8:10], refs[10:18], refs[18]
    copies = [pltpu.make_async_copy(w, h, sems.at[i]) for i, (w, h) in enumerate(zip(given, held))]
    for copy in copies:
        copy.start()
    for i, (copy, ref) in enumerate(zip(copies, held)):
        row = 0 if i % 4 == 0 else row
        copy.wait()
        rows, cols = ref.shape
        for p in range(cols // HEAD):
            outs[i // 4][row : row + rows] = ref[:, HEAD * p : HEAD * (p + 1)]
            row += rows


def pack(*weights):
    return pl.pallas_call(
        pack_kernel,
        out_shape=[shape((PACKED, HEAD))] * 2,
        in_specs=[HBM] * 8,
        out_specs=[VMEM] * 2,
        scratch_shapes=[pltpu.VMEM(w.shape, BF16) for w in weights] + [pltpu.SemaphoreType.DMA((8,))],
        compiler_params=limit(60),
        cost_estimate=cost(0, 8_000_000),
        name="pack",
    )(*weights)


QKV_PART = QKV_PANELS * QKV_ROWS

SLOTS = [(0, 0), (3, 0), (0, 1), (1, 0), (3, 1), (2, 0), (1, 1), (2, 1)]
SLOT_ROWS = 2 * QKV_ROWS
EARLY = 4


def rms(values, gain):
    mean = jnp.sum(values * values, -1, keepdims=True) * (1.0 / D)
    return values * lax.rsqrt(mean + EPSILON) * gain


CHIPS = [(0, 0), (1, 0), (2, 0), (3, 0), (0, 1), (1, 1), (2, 1), (3, 1)]


def chip_index(position, dx, dy):
    x = position // 4
    y = (position // 2) % 2
    return ((x + dx) % 4) * 2 + (y if dy == 0 else 1 - y)


def device_index(position, dx, dy, dc):
    core = position % 2
    return chip_index(position, dx, dy) * 2 + (core if dc == 0 else 1 - core)


def load_qkv(slots, refs, wqkv, sem):
    for slot, sources in enumerate(slots):
        for dc, (piece, row) in enumerate(sources):
            panels = refs[piece].at[pl.ds(row, QKV_PART)].reshape(QKV_PANELS, QKV_ROWS, HEAD)
            to = pl.ds(SLOT_ROWS * slot + QKV_ROWS * dc, QKV_ROWS)
            pltpu.make_async_copy(panels, wqkv.at[:, to], sem).start()


def load_out(position, slots, refs, wo, sem):
    for (dx, dy), sources in zip(SLOTS, slots):
        for dc, (piece, row) in enumerate(sources):
            rows = pl.ds(row + QKV_PART, O_PANELS * O_ROWS)
            panels = refs[piece].at[rows].reshape(O_PANELS, O_ROWS, HEAD)
            owner = device_index(position, dx, dy, dc)
            to = pl.ds(pl.multiple_of(owner * O_ROWS, 16), O_ROWS)
            pltpu.make_async_copy(panels, wo.at[:, to], sem).start()


def wait_for(ref, sem):
    pltpu.make_async_copy(ref, ref, sem).wait()


def causal_mask():
    row = lax.broadcasted_iota(jnp.int32, (SEQ, SEQ), 0)
    col = lax.broadcasted_iota(jnp.int32, (SEQ, SEQ), 1)
    return row >= col


def nt(a, b):
    return lax.dot_general(a, b, (((1,), (1,)), ((), ())), preferred_element_type=F32)


def tn(a, b):
    return lax.dot_general(a, b, (((0,), (0,)), ((), ())), preferred_element_type=F32)


def nn(a, b):
    return jnp.dot(a, b, preferred_element_type=F32)


def probabilities(query, key, causal):
    capped = jnp.tanh(nt(query, key) * (1.0 / (math.sqrt(HEAD) * ATTN_CAP)))
    scores = jnp.where(causal, ATTN_CAP * capped, MASKED)
    top = jnp.max(scores, -1, keepdims=True)
    weights = jnp.where(causal, jnp.exp(scores - top), 0.0)
    return weights / jnp.sum(weights, -1, keepdims=True), capped


def prepare_kernel(pos_ref, x_ref, gains_ref, *refs):
    early, late, n_mine, n_send, turned, ordered = refs
    normed = rms(x_ref[...].astype(F32), gains_ref[0:1, :]).astype(BF16)
    turned[...] = normed.T

    def rows_of(device):
        return turned[pl.ds(pl.multiple_of(device * QKV_ROWS, 16), QKV_ROWS)]

    position = pos_ref[0]
    for slot, (dx, dy) in enumerate(SLOTS):
        for dc in range(2):
            to = SLOT_ROWS * slot + QKV_ROWS * dc
            ordered[to : to + QKV_ROWS] = rows_of(device_index(position, dx, dy, dc))
    early[...] = ordered[0 : SLOT_ROWS * EARLY].T
    late[...] = ordered[SLOT_ROWS * EARLY :].T
    for chip, (dx, dy) in enumerate(CHIPS):
        to = slice(QKV_ROWS * chip, QKV_ROWS * (chip + 1))
        n_mine[to] = rows_of(device_index(position, dx, dy, 0))
        n_send[to] = rows_of(device_index(position, dx, dy, 1))


def early_kernel(slots, normed, *refs):
    pieces, (acc, wqkv, sems) = refs[:-3], refs[-3:]
    half = QKV_PANELS // 2
    for part in range(2):
        panels = pl.ds(half * part, half)
        for slot, sources in enumerate(slots):
            for dc, (piece, row) in enumerate(sources):
                rows = pl.ds(row + THIRD * part, THIRD)
                to = pl.ds(SLOT_ROWS * slot + QKV_ROWS * dc, QKV_ROWS)
                source = pieces[piece].at[rows].reshape(half, QKV_ROWS, HEAD)
                pltpu.make_async_copy(source, wqkv.at[panels, to], sems.at[part]).start()

    def one_panel(p, carry):
        acc[p] = nn(normed[...], wqkv[p])
        return carry

    for part in range(2):
        wait_for(wqkv.at[pl.ds(half * part, half)], sems.at[part])
        lax.fori_loop(half * part, half * (part + 1), one_panel, 0)


def layer(position, early, slots, x_ref, gains_ref, head_ref, normed, acc, pieces, qkv, context, hidden, wqkv, wo, sems, reached=lambda stage: None):
    load_qkv(slots[early:], pieces, wqkv, sems.at[0])
    load_out(position, slots, pieces, wo, sems.at[1])
    reached("loads")
    wait_for(wqkv, sems.at[0])

    def one_panel(p, carry):
        qkv[p] = (acc[p] + nn(normed[...], wqkv[p])).astype(BF16)
        return carry

    lax.fori_loop(0, QKV_PANELS, one_panel, 0)
    reached("qkv")
    causal = causal_mask()
    for h in range(HQ):
        group = h // (HQ // HK)
        probs, _ = probabilities(qkv[h], qkv[HQ + group], causal)
        context[:, HEAD * h : HEAD * (h + 1)] = nn(
            probs.astype(BF16), qkv[HQ + HK + group]
        ).astype(BF16)
    wait_for(wo, sems.at[1])
    reached("out")

    def one_out(p, carry):
        cols = pl.ds(pl.multiple_of(p * HEAD, HEAD), HEAD)
        hidden[:, cols] = x_ref[:, cols].astype(F32) + nn(context[...], wo[p])
        return carry

    lax.fori_loop(0, O_PANELS, one_out, 0)
    reached("hidden")
    final = rms(hidden[...], gains_ref[1:2, :]).astype(BF16)
    logits = LABEL_CAP * jnp.tanh(nn(final, head_ref[...]) * (1.0 / LABEL_CAP))
    return logits, logits - jnp.log(jnp.sum(jnp.exp(logits), -1, keepdims=True))


def own_kernel(slots, pos_ref, x_ref, gains_ref, head_ref, normed, acc, *refs):
    pieces, refs = refs[:-18], refs[-18:]
    c_mine, c_send, qkv_out, hidden_out, logits, wo_out = refs[:6]
    x, head, late, sums, qkv, hidden, context, turned, wqkv, wo, sems, more_sems = refs[6:]
    position = pos_ref[0]

    def copy(source, target, i):
        return pltpu.make_async_copy(source, target, more_sems.at[i])

    reads = [copy(normed, late, 0), copy(acc, sums, 1), copy(x_ref, x, 2), copy(head_ref, head, 3)]
    writes = [copy(qkv, qkv_out, 4), copy(wo, wo_out, 5), copy(hidden, hidden_out, 6)]

    def reached(stage):
        if stage == "loads":
            for read in reads:
                read.start()
            reads[0].wait()
            reads[1].wait()
        if stage == "qkv":
            writes[0].start()
        if stage == "out":
            writes[1].start()
            reads[2].wait()
        if stage == "hidden":
            writes[2].start()
            reads[3].wait()

    logits[...], _ = layer(
        *(position, EARLY, slots, x, gains_ref, head, late, sums, pieces),
        *(qkv, context, hidden, wqkv, wo, sems, reached),
    )
    turned[...] = context[...].T
    for chip, (dx, dy) in enumerate(CHIPS):
        to = slice(O_ROWS * chip, O_ROWS * (chip + 1))
        for dc, out in ((0, c_mine), (1, c_send)):
            at = pl.multiple_of(device_index(position, dx, dy, dc) * O_ROWS, 16)
            out[to] = turned[pl.ds(at, O_ROWS)]
    for write in writes:
        write.wait()


def peer_kernel(
    slots, pos_ref, x_ref, gains_ref, head_ref, normed, acc, labels_ref, own_logits, own_hidden, *refs
):
    pieces, refs = refs[:-8], refs[-8:]
    loss, dhidden, qkv, context, hidden, wqkv, wo, sems = refs
    _, peer_lp = layer(
        pos_ref[0], EARLY, slots, x_ref, gains_ref, head_ref, normed, acc, pieces, qkv, context, hidden, wqkv, wo, sems
    )
    logits = own_logits[...]
    own_lp = logits - jnp.log(jnp.sum(jnp.exp(logits), -1, keepdims=True))
    peer = jnp.exp(peer_lp)
    hot = labels_ref[...] == lax.broadcasted_iota(jnp.int32, (SEQ, LABELS), 1)
    picked = jnp.sum(jnp.where(hot, own_lp, 0.0), -1, keepdims=True)
    loss[...] = jnp.sum(peer * (peer_lp - own_lp), -1, keepdims=True) - picked
    d_lp = (jnp.where(hot, 1.0, 0.0) + peer) * (-1.0 / SEQ)
    d_logits = d_lp - jnp.exp(own_lp) * jnp.sum(d_lp, -1, keepdims=True)
    capped = logits * (1.0 / LABEL_CAP)
    d_raw = (d_logits * (1.0 - capped * capped)).astype(BF16)
    d_final = nt(d_raw, head_ref[...]).astype(BF16).astype(F32) * gains_ref[1:2, :]
    own = own_hidden[...]
    scale = lax.rsqrt(jnp.sum(own * own, -1, keepdims=True) * (1.0 / D) + EPSILON)
    along = jnp.sum(d_final * own, -1, keepdims=True) * (1.0 / D)
    dhidden[...] = (d_final * scale - own * (scale * scale * scale * along)).astype(BF16)


def attention_back_kernel(dhidden, wo_panels, qkv, dqkv, wo, probs, capped, sem):
    for p in range(O_PANELS):
        pltpu.make_async_copy(wo_panels.at[p], wo.at[:, pl.ds(HEAD * p, HEAD)], sem).start()
    causal = causal_mask()
    for h in range(HQ):
        probs[h], capped[h] = probabilities(qkv[h], qkv[HQ + h // (HQ // HK)], causal)
    wait_for(wo, sem)
    for group in range(HK):
        key, value = qkv[HQ + group], qkv[HQ + HK + group]
        d_key = jnp.zeros((SEQ, HEAD), F32)
        d_value = jnp.zeros((SEQ, HEAD), F32)
        for h in range(group * (HQ // HK), (group + 1) * (HQ // HK)):
            d_out = nt(dhidden[...], wo[HEAD * h : HEAD * (h + 1), :]).astype(BF16)
            d_value += tn(probs[h].astype(BF16), d_out)
            d_probs = nt(d_out, value).astype(BF16).astype(F32)
            d_scores = probs[h] * (d_probs - jnp.sum(d_probs * probs[h], -1, keepdims=True))
            slope = (1.0 - capped[h] * capped[h]) * (1.0 / math.sqrt(HEAD))
            d_raw = (d_scores * slope).astype(BF16)
            dqkv[h] = nn(d_raw, key).astype(BF16)
            d_key += tn(d_raw, qkv[h])
        dqkv[HQ + group] = d_key.astype(BF16)
        dqkv[HQ + HK + group] = d_value.astype(BF16)


def store(outs, split, panel, total):
    rows = total.shape[0] // 8
    to = pl.ds(pl.multiple_of(panel * rows, 16), rows)
    for chip, out in enumerate((*outs[:6], split, outs[9])):
        out[to] = total[rows * chip : rows * (chip + 1)]


def hand_out(outs, split):
    for third, out in enumerate(outs[6:9]):
        rows = out.shape[0]
        out[...] = split[rows * third : rows * (third + 1)]


def out_grad_kernel(mine, other, d_mine, d_other, *refs):
    outs, (lhs, rhs, split) = refs[:10], refs[10:]
    lhs[:, 0:SEQ], lhs[:, SEQ : 2 * SEQ] = mine[...], other[...]
    rhs[0:SEQ], rhs[SEQ : 2 * SEQ] = d_mine[...], d_other[...]

    def one_panel(p, carry):
        cols = pl.ds(pl.multiple_of(p * HEAD, HEAD), HEAD)
        store(outs, split, p, nn(lhs[...], rhs[:, cols]).astype(BF16))
        return carry

    lax.fori_loop(0, O_PANELS, one_panel, 0)
    hand_out(outs, split)


def qkv_grad_kernel(mine, other, d_mine, d_other, *refs):
    outs, (lhs, rhs, split) = refs[:10], refs[10:]
    lhs[:, 0:SEQ], lhs[:, SEQ : 2 * SEQ] = mine[...], other[...]
    rhs[:, 0:SEQ], rhs[:, SEQ : 2 * SEQ] = d_mine[...], d_other[...]

    def one_panel(p, carry):
        store(outs, split, p, nn(lhs[...], rhs[p]).astype(BF16))
        return carry

    lax.fori_loop(0, QKV_PANELS, one_panel, 0)
    hand_out(outs, split)


def prepare(position, x, gains):
    return pl.pallas_call(
        prepare_kernel,
        out_shape=[
            shape((SEQ, SLOT_ROWS * count))
            for count in (EARLY, 8 - EARLY)
        ]
        + [shape((D // 2, SEQ))] * 2,
        in_specs=[SMEM, VMEM, VMEM],
        out_specs=[VMEM] * 4,
        scratch_shapes=[pltpu.VMEM((D, SEQ), BF16)] * 2,
        compiler_params=limit(20),
        cost_estimate=cost(10_000_000, 10_000_000),
        name="prepare",
    )(position, x, gains)


def some_wqkv(count):
    return pltpu.VMEM((QKV_PANELS, SLOT_ROWS * count, HEAD), BF16)


def early_pass(normed, arrays, slots):
    return pl.pallas_call(
        functools.partial(early_kernel, slots),
        out_shape=shape((QKV_PANELS, SEQ, HEAD), F32),
        in_specs=[VMEM] + [ANY] * len(arrays),
        out_specs=VMEM,
        scratch_shapes=[some_wqkv(len(slots)), pltpu.SemaphoreType.DMA((2,))],
        compiler_params=limit(14),
        cost_estimate=cost(1_200_000_000, 20_000_000),
        name="early_pass",
    )(normed, *arrays)


def own_pass(position, x, gains, head, normed, acc, arrays, slots):
    return pl.pallas_call(
        functools.partial(own_kernel, slots),
        out_shape=[
            shape((HQ * HEAD // 2, SEQ)),
            shape((HQ * HEAD // 2, SEQ)),
            shape((QKV_PANELS, SEQ, HEAD)),
            shape((SEQ, D), F32),
            shape((SEQ, LABELS), F32),
            shape((O_PANELS, HQ * HEAD, HEAD)),
        ],
        in_specs=[SMEM, ANY, VMEM, ANY, ANY, ANY] + [ANY] * len(arrays),
        out_specs=[VMEM, VMEM, HBM, HBM, VMEM, HBM],
        scratch_shapes=[
            pltpu.VMEM((SEQ, D), BF16),
            pltpu.VMEM((D, LABELS), BF16),
            pltpu.VMEM((SEQ, SLOT_ROWS * (8 - EARLY)), BF16),
            pltpu.VMEM((QKV_PANELS, SEQ, HEAD), F32),
            pltpu.VMEM((QKV_PANELS, SEQ, HEAD), BF16),
            pltpu.VMEM((SEQ, D), F32),
            pltpu.VMEM((SEQ, HQ * HEAD), BF16),
            pltpu.VMEM((HQ * HEAD, SEQ), BF16),
            some_wqkv(8 - EARLY),
            pltpu.VMEM((O_PANELS, HQ * HEAD, HEAD), BF16),
            pltpu.SemaphoreType.DMA((2,)),
            pltpu.SemaphoreType.DMA((7,)),
        ],
        compiler_params=limit(60),
        cost_estimate=cost(3_000_000_000, 30_000_000),
        name="own_pass",
    )(position, x, gains, head, normed, acc, *arrays)


def peer_pass(position, x, gains, head, normed, acc, labels, own_logits, own_hidden, arrays, slots):
    return pl.pallas_call(
        functools.partial(peer_kernel, slots),
        out_shape=[shape((SEQ, 1), F32), shape((SEQ, D))],
        in_specs=[SMEM] + [VMEM] * 8 + [ANY] * len(arrays),
        out_specs=[VMEM] * 2,
        scratch_shapes=[
            pltpu.VMEM((QKV_PANELS, SEQ, HEAD), BF16),
            pltpu.VMEM((SEQ, HQ * HEAD), BF16),
            pltpu.VMEM((SEQ, D), F32),
            some_wqkv(8 - EARLY),
            pltpu.VMEM((O_PANELS, HQ * HEAD, HEAD), BF16),
            pltpu.SemaphoreType.DMA((2,)),
        ],
        compiler_params=limit(26),
        cost_estimate=cost(3_000_000_000, 30_000_000),
        name="peer_pass",
    )(position, x, gains, head, normed, acc, labels, own_logits, own_hidden, *arrays)


def attention_back(dhidden, wo, qkv):
    return pl.pallas_call(
        attention_back_kernel,
        out_shape=shape((QKV_PANELS, SEQ, HEAD)),
        in_specs=[VMEM, HBM, VMEM],
        out_specs=VMEM,
        scratch_shapes=[
            pltpu.VMEM((HQ * HEAD, D), BF16),
            pltpu.VMEM((HQ, SEQ, SEQ), F32),
            pltpu.VMEM((HQ, SEQ, SEQ), F32),
            pltpu.SemaphoreType.DMA,
        ],
        compiler_params=limit(20),
        cost_estimate=cost(2_000_000_000, 16_000_000),
        name="attention_back",
    )(dhidden, wo, qkv)


def weight_grads(kernel, rows, panels, rhs, mine, other, d_mine, d_other, name):
    block = rows * panels
    return pl.pallas_call(
        kernel,
        out_shape=[shape((block, HEAD))] * 6 + [shape((block // 3, HEAD))] * 3 + [shape((block, HEAD))],
        in_specs=[VMEM] * 4,
        out_specs=[VMEM] * 10,
        scratch_shapes=[
            pltpu.VMEM((8 * rows, 2 * SEQ), BF16),
            pltpu.VMEM(rhs, BF16),
            pltpu.VMEM((block, HEAD), BF16),
        ],
        compiler_params=limit(28),
        cost_estimate=cost(2 * 8 * rows * 2 * SEQ * panels * HEAD, 10_000_000),
        name=name,
    )(mine, other, d_mine, d_other)


def third_added_kernel(a2, o3, o1, in_a, in_b, in_c, a2_out, o3_out, o1_out):
    t = in_a.shape[0]
    for third, (value, more, out) in enumerate(
        ((a2, in_a, a2_out), (o3, in_b, o3_out), (o1, in_c, o1_out))
    ):
        for part in range(3):
            rows = slice(t * part, t * (part + 1))
            if part == third:
                out[rows] = (value[rows].astype(F32) + more[...].astype(F32)).astype(BF16)
            else:
                out[rows] = value[rows]


def next_added_kernel(a1, o0, in_x, in_y, in_o0, a1_out, o0_out):
    total = a1[...].astype(F32) + in_x[...].astype(F32) + in_y[...].astype(F32)
    a1_out[...] = total.astype(BF16)
    o0_out[...] = (o0[...].astype(F32) + in_o0[...].astype(F32)).astype(BF16)


def summed_kernel(rows, *refs):
    parts, outs = refs[:4], refs[4:]
    row = 0
    for out in outs:
        for p in range(out.shape[1] // HEAD):
            at = slice(row, row + rows)
            total = parts[0][at].astype(F32)
            for part in parts[1:]:
                total += part[at].astype(F32)
            out[:, HEAD * p : HEAD * (p + 1)] = total
            row += rows


def elementwise(kernel, outs, name, *values):
    return pl.pallas_call(
        kernel,
        out_shape=outs,
        in_specs=[VMEM] * len(values),
        out_specs=[VMEM] * len(outs),
        compiler_params=limit(12),
        cost_estimate=cost(1_000_000, 4_000_000),
        name=name,
    )(*values)


def reduce_first(blocks):
    return moved(blocks[6], to_y), moved(blocks[7], to_prev_x), moved(blocks[8], to_next_x)


def add_thirds(blocks, incoming):
    a2, o3, o1 = blocks[2], blocks[9], blocks[5]
    outs = [shape(a2.shape)] * 3
    return elementwise(third_added_kernel, outs, "add_thirds", a2, o3, o1, *incoming)


def reduce_rest(blocks, added, rows, widths):
    s0, a1, _, a3, o0, *_ = blocks
    a2, o3, o1 = added
    one = shape(s0.shape)
    in_x, in_o0, in_y = together((moved(a2, to_next_x), moved(o3, to_prev_x), moved(o1, to_y)))
    a1, o0 = elementwise(next_added_kernel, [one] * 2, "add_next", a1, o0, in_x, in_y, in_o0)
    last = together((moved(a1, to_next_x), moved(a3, to_prev_x), moved(o0, to_y)))
    outs = [shape((rows, width), F32) for width in widths]
    return elementwise(functools.partial(summed_kernel, rows), outs, "add_last", s0, *last)


def body(
    activations,
    labels,
    own_q,
    own_k,
    own_v,
    own_o,
    peer_q,
    peer_k,
    peer_v,
    peer_o,
    norm_gains,
    label_head,
):
    me = lax.axis_index("fsdp")
    position = me.astype(jnp.int32).reshape(1)
    x = activations[0, 0]
    replicas = lax.axis_size("replica")

    own, peer = pack(
        *(own_q[0], own_k[0], own_v[0], own_o[0]), *(peer_q[0], peer_k[0], peer_v[0], peer_o[0])
    )

    a1, a3 = moved(own, to_prev_x), moved(own, to_next_x)
    peer = lax.ppermute(peer, "replica", [(i, (i + 1) % replicas) for i in range(replicas)])
    s_own = moved(own, to_core)
    *prepared, n_send = prepare(position, x, norm_gains)
    n_other = moved(n_send, to_core)
    column = labels[0, 0].reshape(SEQ, 1)
    a1, a3, own, s_own, n_other, prepared, column = together(
        (a1, a3, own, s_own, n_other, prepared, column)
    )
    n_early, n_late, n_mine = prepared

    y0, a2, p_a3 = moved(own, to_y), moved(a1, to_prev_x), moved(peer, to_next_x)
    s_a1, s_a3 = moved(a1, to_core), moved(a3, to_core)
    y0, a2, p_a3, s_a1, s_a3 = together((y0, a2, p_a3, s_a1, s_a3))

    p_y0, o3, o1 = moved(peer, to_y), moved(y0, to_next_x), moved(y0, to_prev_x)
    s_y0, s_a2 = moved(y0, to_core), moved(a2, to_core)
    p_y0, o3, o1, s_y0, s_a2 = together((p_y0, o3, o1, s_y0, s_a2))

    o2, p_a1, p_o3 = moved(a2, to_y), moved(peer, to_prev_x), moved(p_y0, to_next_x)
    s_o3, s_o1 = moved(o3, to_core), moved(o1, to_core)
    early, s_early = [own, a3, y0, a1], [s_own, s_a3, s_y0, s_a1]
    acc = early_pass(n_early, early + s_early, [((i, 0), (4 + i, 0)) for i in range(4)])
    joined = jnp.concatenate([peer, p_a3, p_y0], 0)
    o2, p_a1, p_o3, s_o3, s_o1, joined, acc = together((o2, p_a1, p_o3, s_o3, s_o1, joined, acc))

    p_o1, p_a2, p_o2 = moved(p_a1, to_y), moved(p_a1, to_prev_x), moved(p_o3, to_next_x)
    s_o2, s_joined = moved(o2, to_core), moved(joined, to_core)
    s_p_a1 = moved(p_a1, to_core)
    c_mine, c_send, qkv, hidden, logits, wo = own_pass(
        position,
        x,
        norm_gains,
        label_head,
        n_late,
        acc,
        early + [o3, a2, o1, o2] + s_early + [s_o3, s_a2, s_o1, s_o2],
        [((i, 0), (8 + i, 0)) for i in range(8)],
    )
    p_o1, p_a2, p_o2, s_joined, s_p_a1, c_send, hidden = together(
        (p_o1, p_a2, p_o2, s_joined, s_p_a1, c_send, hidden)
    )

    late = [p_o3, p_a2, p_o1, p_o2]
    s_late = [moved(piece, to_core) for piece in late]
    c_other = moved(c_send, to_core)
    arrays = [peer, p_a3, p_y0, p_a1, s_joined, s_p_a1]
    slots = [((i, 0), (4, PACKED * i)) for i in range(3)] + [((3, 0), (5, 0))]
    p_acc = early_pass(n_early, arrays, slots)
    loss, dhidden = peer_pass(
        position,
        x,
        norm_gains,
        label_head,
        n_late,
        p_acc,
        column,
        logits,
        hidden,
        arrays + late + s_late,
        slots + [((6 + i, 0), (10 + i, 0)) for i in range(4)],
    )
    dhidden, c_other = together((dhidden, c_other))
    d_other = moved(dhidden, to_core)
    dqkv = attention_back(dhidden, wo, qkv)
    dqkv_other = moved(dqkv, to_core)
    out_blocks = weight_grads(
        out_grad_kernel,
        *(O_ROWS, O_PANELS, (2 * SEQ, D)),
        *(c_mine, c_other, dhidden, d_other, "out_grads"),
    )
    dqkv, dqkv_other, *out_blocks = together((dqkv, dqkv_other, *out_blocks))
    qkv_blocks = weight_grads(
        qkv_grad_kernel,
        *(QKV_ROWS, QKV_PANELS, (QKV_PANELS, 2 * SEQ, HEAD)),
        *(n_mine, n_other, dqkv, dqkv_other, "qkv_grads"),
    )
    in_a, in_b, in_c, *qkv_blocks = together((*reduce_first(out_blocks), *qkv_blocks))
    added = add_thirds(out_blocks, (in_a, in_b, in_c))
    (grad_out,) = reduce_rest(out_blocks, added, O_ROWS, [D])
    added = add_thirds(qkv_blocks, together(reduce_first(qkv_blocks)))
    grads = reduce_rest(qkv_blocks, added, QKV_ROWS, [HQ * HEAD, HK * HEAD, HK * HEAD])
    return (loss.reshape(1, 1, SEQ), *[grad[None] for grad in grads], grad_out[None])


def solution(mesh):
    weights = P("replica", "fsdp", None)
    return jax.shard_map(
        body,
        mesh=mesh,
        in_specs=(P("replica", "fsdp", None, None), weights, *([weights] * 8), P(), P()),
        out_specs=(weights,) * 5,
        check_vma=False,
    )
```
